128 devices in a mesh: group: 4 (over y), queue: 32 (over z, x, core).
Axes of the slice: x: 4, y: 4, z: 4, core: 2. Of those that a mesh axis runs over, the one named last changes fastest.
Arguments:
- queries: bfloat16 [32, 64, 128], P('queue', 'group'), may hold values from -4 to 4
- positive: int32 [64], replicated, may hold values from 0 to 16383
- queue: bfloat16 [16384, 96, 128], P(('group', 'queue')), may hold values from -4 to 4
- slot_order: int32 [16384], P(('group', 'queue')), may hold values from 0 to 16383, each once
Outputs:
- loss: float32 [], replicated
- query_grad: float32 [32, 64, 128], P('queue', 'group')
The draws below stay inside these ranges and needn't reach their ends.
Inputs may be any that keep to these rules, and one draw needn't show every extreme that they name: `slot_order`: every id of 0 to 16383 stands in exactly one slot.
All inputs are finite; a program needn't handle non-finite values.
Results may differ from the reference program's by a relative error of at most 0.017.
Values may be sent and summed in bfloat16 or wider, within the bound.
A program may use at most 64 MiB of HBM per device.

```python
import jax
import jax.numpy as jnp
from jax import lax

DIM = 128
LQ = 32
LD = 96
NQ_DEV = 128
B = 64
NQ = 16384


def normal_table(key):
    return jnp.clip(jax.random.normal(key, (NQ, LD, DIM), jnp.float32), -4.0, 4.0)


def draw_queue(key, part):
    table = normal_table(key)
    return table.astype(jnp.bfloat16)


def draw_queries(key, part):
    key = jax.random.fold_in(key, 7)
    values = jnp.clip(jax.random.normal(key, (LQ, B, DIM), jnp.float32), -4.0, 4.0)
    return values.astype(jnp.bfloat16)


def plant(values, stream_key, smallest, largest):
    spot = [jax.random.randint(jax.random.fold_in(stream_key, axis), (), 0, length) for axis, length in enumerate(values.shape)]
    widest = values.shape.index(max(values.shape))
    beside = spot[:widest] + [(spot[widest] + 1) % values.shape[widest]] + spot[widest + 1:]
    return values.at[tuple(spot)].set(smallest).at[tuple(beside)].set(largest)


def setup_inputs(seed: int = 0) -> dict:
    seeds = jax.random.split(jax.random.key(seed), 5)
    return {
        "queries": draw_queries(jax.random.fold_in(seeds[4], 71), 0),
        "positive": plant(jax.random.randint(seeds[1], (B,), 0, NQ), jax.random.fold_in(seeds[1], 1), 0, NQ - 1).astype(jnp.int32),
        "queue": draw_queue(jax.random.fold_in(seeds[4], 71), 0),
        "slot_order": jax.random.permutation(seeds[3], NQ).astype(jnp.int32),
    }


sharpness = 0.1
softness_divisor = 0.05
epsilon = 1e-06

def unit_vectors(values):
    wide = values.astype(jnp.float32)
    length = jnp.sqrt(lax.optimization_barrier(jnp.sum(wide * wide, axis=-1, keepdims=True)) + epsilon)
    return (wide / length, length)

def token_terms(query_block, documents):
    dots = jnp.einsum('tbk,djk->tbjd', query_block.astype(jnp.float32), documents.astype(jnp.float32))
    powered = jnp.exp(dots / sharpness)
    return (powered, lax.optimization_barrier(jnp.sum(powered, axis=2)))

def reference(queries, positive, queue, slot_order):
    query_unit, query_length = unit_vectors(queries)
    query_half = query_unit.astype(jnp.bfloat16)
    doc_half = unit_vectors(queue)[0].astype(jnp.bfloat16)
    block_count = NQ // NQ_DEV
    doc_blocks = doc_half.reshape(block_count, NQ_DEV, LD, DIM)

    def block_scores(documents):
        similarity_scores = jnp.zeros((B, NQ_DEV), jnp.float32)
        for first in range(0, LQ, 2):
            powered, summed = token_terms(query_half[first:first + 2], documents)
            similarity_scores = similarity_scores + lax.optimization_barrier(jnp.sum(sharpness * jnp.log(summed), axis=0))
        return similarity_scores
    similarity_scores = lax.map(block_scores, doc_blocks)
    similarity_scores = jnp.transpose(similarity_scores, (1, 0, 2)).reshape(B, NQ)
    scaled_logits = similarity_scores / softness_divisor
    positive_match = slot_order[None, :] == positive[:, None]
    target = lax.optimization_barrier(jnp.sum(jnp.where(positive_match, scaled_logits, 0.0), axis=1))
    top = lax.optimization_barrier(jnp.max(scaled_logits, axis=1))
    log_partition = top + jnp.log(lax.optimization_barrier(jnp.sum(jnp.exp(scaled_logits - top[:, None]), axis=1)))
    loss = jnp.mean(log_partition - target)
    softmax_factor = (jnp.exp(scaled_logits - log_partition[:, None]) - positive_match.astype(jnp.float32)) / softness_divisor
    coef_blocks = jnp.transpose(softmax_factor.reshape(B, block_count, NQ_DEV), (1, 0, 2))

    def add_block(carry, pair):
        documents, block_coef = pair
        pieces = []
        for first in range(0, LQ, 2):
            powered, summed = token_terms(query_half[first:first + 2], documents)
            weights = (block_coef[None, :, None, :] * powered / summed[:, :, None, :]).astype(jnp.bfloat16)
            pieces.append(jnp.einsum('tbjd,djk->tbk', weights.astype(jnp.float32), documents.astype(jnp.float32)))
        return (carry + jnp.concatenate(pieces, axis=0), None)
    unit_grad, _ = lax.scan(add_block, jnp.zeros((LQ, B, DIM), jnp.float32), (doc_blocks, coef_blocks))
    query_grad = (unit_grad - query_unit * lax.optimization_barrier(jnp.sum(query_unit * unit_grad, axis=-1, keepdims=True))) / query_length
    return (loss, query_grad)
```

```python
import functools

import jax
import jax.numpy as jnp
from jax import lax
from jax.experimental import pallas as pl
from jax.experimental.pallas import tpu as pltpu
from jax.sharding import PartitionSpec as P

sharpness = 0.1
softness_divisor = 0.05
epsilon = 1e-06
log2e = 1.4426950408889634
MESH = pl.DeviceIdType.MESH
ROWS = 16
HALF = 8


def first_order(k, group):
    own = lax.div(4 - k, 4)
    other = (k - 1) + lax.div(k + 3 - group, 4)
    return own * group + (1 - own) * other


def last_order(k, group, groups):
    own = lax.div(k, groups - 1)
    other = k + lax.div(k - group + 4, 4)
    return own * group + (1 - own) * other


def kernel(
    groups, tokens, docs, length, chunks, vmem,
    pos_ref, q_ref, slot_ref, queue_ref,
    grad_ref, loss_ref,
    powered, doc, doc_t, qbuf, sums, logits, coef, slot_col, st1, st2, fin, gsend, grecv, yrecv, partial,
    load_sem, qy_recv, q_recv, s1_recv, s2_recv, g_recv, y_recv, send_sem,
):
    group = lax.axis_index("group")
    me = lax.axis_index("queue")
    rows = docs * length
    lanes = HALF * tokens
    chunk = rows // chunks
    blocks = 4
    block_rows = rows // blocks

    def load(c):
        part = pl.ds(c * chunk, chunk)
        return pltpu.make_async_copy(queue_ref.at[part], doc.at[part], load_sem.at[c])

    for c in range(chunks):
        load(c).start()

    def peer_of(j):
        return lax.rem(me + j, tokens)

    def other_group(j):
        return lax.rem(group + j, groups)

    barrier = pltpu.get_barrier_semaphore()

    def greet(j, carry):
        pl.semaphore_signal(barrier, inc=1, device_id={"queue": peer_of(j)}, device_id_type=MESH)
        return carry

    lax.fori_loop(1, tokens, greet, 0)
    for j in range(1, groups):
        pl.semaphore_signal(barrier, inc=1, device_id={"group": other_group(j)}, device_id_type=MESH)

    wide = q_ref[...].astype(jnp.float32)
    q_length = jnp.sqrt(jnp.sum(wide * wide, axis=-1, keepdims=True) + epsilon)
    q_unit = wide / q_length
    qbuf[group * tokens + me] = q_unit.astype(jnp.bfloat16)
    slot_col[...] = jnp.broadcast_to(slot_ref[...].astype(jnp.float32), (128, docs)).T

    pl.semaphore_wait(barrier, tokens - 1 + groups - 1)

    def to_group(src, dst, send, recv, j):
        return pltpu.make_async_remote_copy(
            src_ref=src, dst_ref=dst, send_sem=send, recv_sem=recv,
            device_id={"group": j}, device_id_type=MESH,
        )

    def to_peer(src, dst, send, recv, j):
        return pltpu.make_async_remote_copy(
            src_ref=src, dst_ref=dst, send_sem=send, recv_sem=recv,
            device_id={"queue": j}, device_id_type=MESH,
        )

    def wait_in(ref, sem):
        to_peer(ref, ref, send_sem.at[0], sem, me).wait_recv()

    def wait_out(ref, sem):
        to_peer(ref, ref, sem, q_recv.at[0], me).wait_send()

    mine = qbuf.at[group * tokens + me]
    for j in range(1, groups):
        to_group(mine, mine, send_sem.at[0], qy_recv.at[group], other_group(j)).start()

    def spread(g):
        block = qbuf.at[g * tokens + me]

        def body(j, carry):
            to_peer(block, block, send_sem.at[0], q_recv.at[g], peer_of(j)).start()
            return carry

        lax.fori_loop(1, tokens, body, 0)

    spread(group)

    def normalize(c):
        load(c).wait()
        part = pl.ds(c * chunk, chunk)
        x = doc[part, :].astype(jnp.float32)
        y = x * lax.rsqrt(jnp.sum(x * x, axis=-1, keepdims=True) + epsilon)
        doc[part, :] = y.astype(jnp.bfloat16)
        doc_t[:, part] = y.T.astype(jnp.bfloat16)

    def pass_on(j):
        g = other_group(j)
        block = qbuf.at[g * tokens + me]
        wait_in(block, qy_recv.at[g])
        spread(g)

    for c in range(chunks):
        normalize(c)
        if c == chunks // 2:
            for j in range(1, groups):
                pass_on(j)

    lane = lax.broadcasted_iota(jnp.int32, (1, 128), 1)
    lane = lax.rem(lane, HALF)

    def hits(t):
        wanted = jnp.zeros((1, 128), jnp.float32)
        for b in range(HALF):
            wanted = jnp.where(lane == b, pos_ref[t * HALF + b].astype(jnp.float32), wanted)
        return slot_col[...] == wanted

    def score_tile(g, h):
        t = g * 2 + h
        q = qbuf[pl.ds(g * tokens, tokens)].astype(jnp.float32)
        q = jnp.where(h == 0, q[:, :HALF], q[:, HALF:])
        q = q.reshape(lanes, 128).T.astype(jnp.bfloat16)
        for c in range(blocks):
            part = pl.ds(c * block_rows, block_rows)
            x = jnp.dot(doc[part, :], q, preferred_element_type=jnp.float32)
            e = jnp.exp2(x * (log2e / sharpness))
            powered[t, part, :] = e.astype(jnp.bfloat16)
            summed = jnp.sum(e.reshape(docs // blocks, length, lanes), axis=1)
            sums[t, c * (docs // blocks):(c + 1) * (docs // blocks), :] = summed
        score = jnp.log(sums[t]) * (sharpness / softness_divisor)
        total = score[:, :128]
        for c in range(1, lanes // 128):
            total = total + score[:, c * 128:(c + 1) * 128]
        for shift in (8, 16, 32, 64):
            total = total + pltpu.roll(total, shift, 1)
        logits[t] = total
        top = jnp.max(total, axis=0, keepdims=True)
        row = g * tokens + me
        st1[row, pl.ds(h, 1), :] = top
        st1[row, pl.ds(4 + h, 1), :] = jnp.sum(jnp.exp(total - top), axis=0, keepdims=True)
        st1[row, pl.ds(6 + h, 1), :] = jnp.sum(jnp.where(hits(t), total, 0.0), axis=0, keepdims=True)

    def combine(parts):
        top = jnp.max(parts, axis=0)
        scale = jnp.exp(pltpu.roll(parts, 4, 1) - pltpu.roll(top, 4, 0)[None])
        row = lax.broadcasted_iota(jnp.int32, (8, 128), 0)
        return jnp.where(row < 4, top, jnp.sum(parts * scale, axis=0))

    def send_stats(g):
        block = st1.at[g * tokens + me]

        def body(j, carry):
            to_peer(block, block, send_sem.at[1], s1_recv.at[g], peer_of(j)).start()
            return carry

        lax.fori_loop(1, tokens, body, 0)

    def combine_plane(g):
        wait_in(st1.at[pl.ds(0, tokens - 1)], s1_recv.at[g])
        block = st2.at[g * groups + group]
        st2[g * groups + group] = combine(st1[pl.ds(g * tokens, tokens)])
        for j in range(1, groups):
            to_group(block, block, send_sem.at[2], s2_recv.at[g], other_group(j)).start()

    def combine_groups(g):
        wait_in(st2.at[pl.ds(0, groups - 1)], s2_recv.at[g])
        fin[g] = combine(st2[pl.ds(g * groups, groups)])

    def pass_a(k, carry):
        g = first_order(k, group)

        @pl.when(k > 0)
        def _():
            wait_in(qbuf.at[pl.ds(0, tokens - 1)], q_recv.at[g])

        def tile(h, c):
            score_tile(g, h)
            return c

        lax.fori_loop(0, 2, tile, 0)
        send_stats(g)

        @pl.when(k > 0)
        def _():
            combine_plane(first_order(k - 1, group))

        return carry

    wait_in(qbuf.at[pl.ds(0, tokens - 1)], q_recv.at[group])
    zero = jnp.zeros((2, 128), jnp.float32)

    def clear(g, carry):
        st1[g * tokens + me, 2:4, :] = zero
        return carry

    lax.fori_loop(0, groups, clear, 0)
    lax.fori_loop(0, groups, pass_a, 0)
    combine_plane(first_order(jnp.int32(groups - 1), group))

    def weight_tile(g, h):
        t = g * 2 + h
        lse = fin[g, pl.ds(h, 1), :] + jnp.log(fin[g, pl.ds(4 + h, 1), :])
        c = (jnp.exp(logits[t] - lse) - hits(t).astype(jnp.float32)) / softness_divisor
        c = jnp.concatenate([c] * (lanes // 128), axis=1)
        coef[...] = c / sums[t]
        out = jnp.zeros((128, lanes), jnp.float32)
        for b in range(blocks):
            part = pl.ds(b * block_rows, block_rows)
            c = coef[b * (docs // blocks):(b + 1) * (docs // blocks), :].astype(jnp.bfloat16)
            w = jnp.broadcast_to(c[:, None, :], (docs // blocks, length, lanes)).reshape(block_rows, lanes)
            w = powered[t, part, :] * w
            out = out + jnp.dot(doc_t[:, part], w, preferred_element_type=jnp.float32)
        partial[h] = out.T.reshape(tokens, HALF, 128)

    def send_grad(g):
        def body(j, carry):
            peer = peer_of(j)
            to_peer(
                gsend.at[g * tokens + peer], grecv.at[g * tokens + me], send_sem.at[3], g_recv.at[g], peer
            ).start()
            return carry

        lax.fori_loop(1, tokens, body, 0)

    def plane_sum(g):
        wait_in(grecv.at[pl.ds(0, tokens - 1)], g_recv.at[g])
        return jnp.sum(grecv[pl.ds(g * tokens, tokens)].astype(jnp.float32), axis=0)

    def pass_b(k, carry):
        g = last_order(k, group, groups)
        combine_groups(g)

        def tile(h, c):
            weight_tile(g, h)
            return c

        lax.fori_loop(0, 2, tile, 0)
        both = jnp.concatenate([partial[0], partial[1]], axis=1)
        gsend[pl.ds(g * tokens, tokens)] = both.astype(jnp.bfloat16)
        grecv[g * tokens + me] = gsend[g * tokens + me]
        send_grad(g)

        @pl.when(k > 0)
        def _():
            before = last_order(k - 1, group, groups)
            block = yrecv.at[group * groups + before]
            yrecv[group * groups + before] = plane_sum(before)
            to_group(block, yrecv.at[group * groups + before], send_sem.at[4], y_recv, before).start()

        return carry

    lax.fori_loop(0, groups, pass_b, 0)

    loss = jnp.zeros((2, 128), jnp.float32)
    for g in range(groups):
        loss = loss + (fin[g, 0:2, :] + jnp.log(fin[g, 4:6, :]) - fin[g, 6:8, :])
    scale = 1.0 / ((128 // HALF) * groups * ROWS)
    loss_ref[...] = jnp.sum(jnp.sum(loss, axis=0, keepdims=True), axis=1, keepdims=True) * scale

    grad = plane_sum(group)
    if groups > 1:
        wait_in(yrecv.at[pl.ds(0, groups - 1)], y_recv)
        for j in range(1, groups):
            grad = grad + yrecv[other_group(j) * groups + group]
    along = jnp.sum(q_unit * grad, axis=-1, keepdims=True)
    grad_ref[...] = (grad - q_unit * along) / q_length

    many = groups * (tokens - 1)
    wait_out(qbuf.at[pl.ds(0, many + groups - 1)], send_sem.at[0])
    wait_out(st1.at[pl.ds(0, many)], send_sem.at[1])
    wait_out(gsend.at[pl.ds(0, many)], send_sem.at[3])
    if groups > 1:
        wait_out(st2.at[pl.ds(0, groups * (groups - 1))], send_sem.at[2])
        wait_out(yrecv.at[pl.ds(0, groups - 1)], send_sem.at[4])


def on_device(groups, tokens, queries, positive, queue, slot_order):
    docs, length, dim = queue.shape
    rows = docs * length
    lanes = HALF * tokens
    vmem = 63 * 2**20
    VM = pl.BlockSpec(memory_space=pltpu.VMEM)
    chunks = 8 if docs % 8 == 0 else 1
    f32, bf16 = jnp.float32, jnp.bfloat16
    DMA = pltpu.SemaphoreType.DMA
    grad, loss = pl.pallas_call(
        functools.partial(kernel, groups, tokens, docs, length, chunks, vmem),
        out_shape=(jax.ShapeDtypeStruct((ROWS, dim), f32), jax.ShapeDtypeStruct((1, 1), f32)),
        in_specs=[pl.BlockSpec(memory_space=pltpu.SMEM), VM, VM, pl.BlockSpec(memory_space=pl.ANY)],
        out_specs=(VM, VM),
        scratch_shapes=[
            pltpu.VMEM((2 * groups, rows, lanes), bf16),
            pltpu.VMEM((rows, dim), bf16),
            pltpu.VMEM((dim, rows), bf16),
            pltpu.VMEM((groups * tokens, ROWS, dim), bf16),
            pltpu.VMEM((2 * groups, docs, lanes), f32),
            pltpu.VMEM((2 * groups, docs, 128), f32),
            pltpu.VMEM((docs, lanes), f32),
            pltpu.VMEM((docs, 128), f32),
            pltpu.VMEM((groups * tokens, 8, 128), f32),
            pltpu.VMEM((groups * groups, 8, 128), f32),
            pltpu.VMEM((groups, 8, 128), f32),
            pltpu.VMEM((groups * tokens, ROWS, dim), bf16),
            pltpu.VMEM((groups * tokens, ROWS, dim), bf16),
            pltpu.VMEM((groups * groups, ROWS, dim), f32),
            pltpu.VMEM((2, tokens, HALF, dim), f32),
            DMA((chunks,)),
            DMA((groups,)),
            DMA((groups,)),
            DMA((groups,)),
            DMA((groups,)),
            DMA((groups,)),
            DMA,
            DMA((5,)),
        ],
        compiler_params=pltpu.CompilerParams(
            collective_id=0, has_side_effects=True, vmem_limit_bytes=vmem
        ),
    )(positive, queries.reshape(ROWS, dim), slot_order.reshape(1, docs), queue.reshape(rows, dim))
    return loss.reshape(()), grad.reshape(1, ROWS, dim)


def solution(mesh):
    groups, tokens = mesh.shape["group"], mesh.shape["queue"]
    return jax.shard_map(
        functools.partial(on_device, groups, tokens),
        mesh=mesh,
        in_specs=(
            P("queue", "group", None),
            P(),
            P(("group", "queue"), None, None),
            P(("group", "queue")),
        ),
        out_specs=(P(), P("queue", "group", None)),
        check_vma=False,
    )
```

```python
import functools

import jax
import jax.numpy as jnp
from jax import lax
from jax.experimental import pallas as pl
from jax.experimental.pallas import tpu as pltpu
from jax.sharding import PartitionSpec as P

sharpness = 0.1
softness_divisor = 0.05
epsilon = 1e-06
log2e = 1.4426950408889634
MESH = pl.DeviceIdType.MESH
ROWS = 16
HALF = 8
SUB = 8


def first_order(k, group):
    own = lax.div(4 - k, 4)
    other = (k - 1) + lax.div(k + 3 - group, 4)
    return own * group + (1 - own) * other


def last_order(k, group, groups):
    own = lax.div(k, groups - 1)
    other = k + lax.div(k - group + 4, 4)
    return own * group + (1 - own) * other


def kernel(
    groups, tokens, docs, length, chunks, vmem,
    pos_ref, q_ref, slot_ref, queue_ref,
    grad_ref, loss_ref,
    powered, doc, doc_t, qbuf, sums, logits, slot_col, st1, st2, fin, gsend, grecv, yrecv,
    load_sem, qy_recv, q_recv, s1_recv, s2_recv, g_recv, y_recv, send_sem,
):
    group = lax.axis_index("group")
    me = lax.axis_index("queue")
    rows = docs * length
    lanes = HALF * tokens
    chunk = rows // chunks
    blocks = 8
    block_rows = rows // blocks
    block_docs = docs // blocks

    def load(c):
        part = pl.ds(c * chunk, chunk)
        return pltpu.make_async_copy(queue_ref.at[part], doc.at[part], load_sem.at[c])

    for c in range(chunks):
        load(c).start()

    def peer_of(j):
        return lax.rem(me + j, tokens)

    def other_group(j):
        return lax.rem(group + j, groups)

    barrier = pltpu.get_barrier_semaphore()

    for j in range(1, tokens):
        pl.semaphore_signal(barrier, inc=1, device_id={"queue": peer_of(j)}, device_id_type=MESH)
    for j in range(1, groups):
        pl.semaphore_signal(barrier, inc=1, device_id={"group": other_group(j)}, device_id_type=MESH)

    wide = q_ref[...].astype(jnp.float32)
    q_length = jnp.sqrt(jnp.sum(wide * wide, axis=-1, keepdims=True) + epsilon)
    q_unit = wide / q_length
    qbuf[group * tokens + me] = q_unit.astype(jnp.bfloat16)
    slot_col[...] = jnp.broadcast_to(slot_ref[...].astype(jnp.float32), (128, docs)).T

    pl.semaphore_wait(barrier, tokens - 1 + groups - 1)

    def to_group(src, dst, send, recv, j):
        return pltpu.make_async_remote_copy(
            src_ref=src, dst_ref=dst, send_sem=send, recv_sem=recv,
            device_id={"group": j}, device_id_type=MESH,
        )

    def to_peer(src, dst, send, recv, j):
        return pltpu.make_async_remote_copy(
            src_ref=src, dst_ref=dst, send_sem=send, recv_sem=recv,
            device_id={"queue": j}, device_id_type=MESH,
        )

    def wait_in(ref, sem):
        to_peer(ref, ref, send_sem.at[0], sem, me).wait_recv()

    def wait_out(ref, sem):
        to_peer(ref, ref, sem, q_recv.at[0], me).wait_send()

    mine = qbuf.at[group * tokens + me]
    for j in range(1, groups):
        to_group(mine, mine, send_sem.at[0], qy_recv.at[group], other_group(j)).start()

    def to_all(src_of, dst, send, recv):
        for j in range(1, tokens):
            peer = peer_of(j)
            to_peer(src_of(peer), dst, send, recv, peer).start()

    def spread(g):
        block = qbuf.at[g * tokens + me]
        to_all(lambda peer: block, block, send_sem.at[0], q_recv.at[g])

    spread(group)

    def normalize(c):
        load(c).wait()
        part = pl.ds(c * chunk, chunk)
        x = doc[part, :].astype(jnp.float32)
        y = x * lax.rsqrt(jnp.sum(x * x, axis=-1, keepdims=True) + epsilon)
        y = y.reshape(chunk // (SUB * length), SUB, length, 128).swapaxes(1, 2).reshape(chunk, 128)
        doc[part, :] = y.astype(jnp.bfloat16)
        doc_t[:, part] = y.T.astype(jnp.bfloat16)

    def pass_on(j):
        g = other_group(j)
        block = qbuf.at[g * tokens + me]
        wait_in(block, qy_recv.at[g])
        spread(g)

    for c in range(chunks):
        normalize(c)
        if c == chunks // 2:
            for j in range(1, groups):
                pass_on(j)

    lane = lax.broadcasted_iota(jnp.int32, (1, 128), 1)
    spot = lax.rem(lane, HALF)
    field = lax.div(lane, HALF)

    def hits(t):
        wanted = jnp.zeros((1, 128), jnp.float32)
        for b in range(HALF):
            wanted = jnp.where(spot == b, pos_ref[t * HALF + b].astype(jnp.float32), wanted)
        return slot_col[...] == wanted

    def everywhere(x):
        for shift in (8, 16, 32, 64):
            x = x + pltpu.roll(x, shift, 1)
        return x

    def query_tile(g, h):
        q = qbuf[pl.ds(g * tokens, tokens)].astype(jnp.float32)[:, h * HALF:(h + 1) * HALF]
        return q.reshape(lanes, 128).T.astype(jnp.bfloat16)

    def dots(g, h):
        t = g * 2 + h
        q = query_tile(g, h)
        for c in range(blocks):
            part = pl.ds(c * block_rows, block_rows)
            x = jnp.dot(doc[part, :], q, preferred_element_type=jnp.float32)
            e = jnp.exp2(x * (log2e / sharpness))
            powered[t, part, :] = e.astype(jnp.bfloat16)
            summed = jnp.sum(e.reshape(block_docs // SUB, length, SUB, lanes), axis=1)
            sums[t, c * block_docs:(c + 1) * block_docs, :] = summed.reshape(block_docs, lanes)

    def scores(g, h):
        t = g * 2 + h
        score = jnp.log(sums[t]) * (sharpness / softness_divisor)
        total = score[:, :128]
        for c in range(1, lanes // 128):
            total = total + score[:, c * 128:(c + 1) * 128]
        total = everywhere(total)
        logits[t] = total
        top = jnp.max(total, axis=0, keepdims=True)
        mass = jnp.sum(jnp.exp(total - top), axis=0, keepdims=True)
        target = jnp.sum(jnp.where(hits(t), total, 0.0), axis=0, keepdims=True)
        row = jnp.where(field == h, top, 0.0)
        row = jnp.where(field == 4 + h, mass, row)
        row = jnp.where(field == 6 + h, target, row)
        at = g * tokens + me
        if h == 0:
            st1[at] = row
        else:
            st1[at] = st1[at] + row

    def combine(parts):
        top = jnp.max(parts, axis=0)
        shifted = pltpu.roll(parts.reshape(-1, 128), 32, 1).reshape(parts.shape)
        scale = jnp.exp(shifted - pltpu.roll(top, 32, 1)[None])
        return jnp.where(field < 4, top, jnp.sum(parts * scale, axis=0))

    def send_stats(g):
        block = st1.at[g * tokens + me]
        to_all(lambda peer: block, block, send_sem.at[1], s1_recv.at[g])

    def combine_plane(g):
        wait_in(st1.at[pl.ds(0, tokens - 1)], s1_recv.at[g])
        block = st2.at[g * groups + group]
        st2[g * groups + group] = combine(st1[pl.ds(g * tokens, tokens)])
        for j in range(1, groups):
            to_group(block, block, send_sem.at[2], s2_recv.at[g], other_group(j)).start()

    def combine_groups(g):
        wait_in(st2.at[pl.ds(0, groups - 1)], s2_recv.at[g])
        fin[g] = combine(st2[pl.ds(g * groups, groups)])

    def pass_a(k, carry):
        g = first_order(k, group)
        before = first_order(k - 1 + lax.div(4 - k, 4), group)

        @pl.when(k > 0)
        def _():
            wait_in(qbuf.at[pl.ds(0, tokens - 1)], q_recv.at[g])

        scores(before, 1)
        dots(g, 0)

        @pl.when(k > 0)
        def _():
            send_stats(before)

        scores(g, 0)
        dots(g, 1)

        @pl.when(k > 0)
        def _():
            combine_plane(before)

        return carry

    sums[group * 2 + 1] = jnp.ones((docs, lanes), jnp.float32)
    st1[group * tokens + me] = jnp.zeros((1, 128), jnp.float32)
    wait_in(qbuf.at[pl.ds(0, tokens - 1)], q_recv.at[group])
    lax.fori_loop(0, groups, pass_a, 0)
    last = first_order(jnp.int32(groups - 1), group)
    scores(last, 1)
    send_stats(last)

    def weight(g, h):
        t = g * 2 + h
        row = fin[g]
        lse = row + jnp.log(pltpu.roll(row, 96, 1))
        lse = everywhere(jnp.where(field == h, lse, 0.0))
        c = (jnp.exp(logits[t] - lse) - hits(t).astype(jnp.float32)) / softness_divisor
        c = jnp.concatenate([c] * (lanes // 128), axis=1)
        return c / sums[t]

    def gradient(g, h, c):
        t = g * 2 + h
        out = jnp.zeros((128, lanes), jnp.float32)
        for b in range(blocks):
            part = pl.ds(b * block_rows, block_rows)
            w = []
            for d in range(b * block_docs, (b + 1) * block_docs, SUB):
                twice = jnp.concatenate([c[d:d + SUB]] * 2, axis=0).astype(jnp.bfloat16)
                p = powered[t, pl.ds(d * length, SUB * length), :]
                w.append((p.reshape(length // 2, 2 * SUB, lanes) * twice[None]).reshape(SUB * length, lanes))
            w = jnp.concatenate(w, axis=0)
            out = out + jnp.dot(doc_t[:, part], w, preferred_element_type=jnp.float32)
        return out.T.reshape(tokens, HALF, 128)

    def plane_sum(g):
        wait_in(grecv.at[pl.ds(0, tokens - 1)], g_recv.at[g])
        return jnp.sum(grecv[pl.ds(g * tokens, tokens)].astype(jnp.float32), axis=0)

    def pass_b(k, carry):
        g = last_order(k, group, groups)
        combine_groups(g)
        c = [weight(g, h) for h in range(2)]
        both = jnp.concatenate([gradient(g, h, c[h]) for h in range(2)], axis=1)
        gsend[pl.ds(g * tokens, tokens)] = both.astype(jnp.bfloat16)
        grecv[g * tokens + me] = gsend[g * tokens + me]
        to_all(lambda peer: gsend.at[g * tokens + peer], grecv.at[g * tokens + me], send_sem.at[3], g_recv.at[g])

        @pl.when(k == 0)
        def _():
            combine_plane(last)

        @pl.when(k > 0)
        def _():
            before = last_order(k - 1, group, groups)
            block = yrecv.at[group * groups + before]
            yrecv[group * groups + before] = plane_sum(before)
            to_group(block, block, send_sem.at[4], y_recv, before).start()

        return carry

    lax.fori_loop(0, groups, pass_b, 0)

    loss = jnp.zeros((1, 128), jnp.float32)
    for g in range(groups):
        row = fin[g]
        loss = loss + (row + jnp.log(pltpu.roll(row, 96, 1)) - pltpu.roll(row, 80, 1))
    loss = jnp.sum(jnp.where(field < 2, loss, 0.0), axis=1, keepdims=True)
    loss_ref[...] = loss * (1.0 / (groups * ROWS))

    grad = plane_sum(group)
    if groups > 1:
        wait_in(yrecv.at[pl.ds(0, groups - 1)], y_recv)
        for j in range(1, groups):
            grad = grad + yrecv[other_group(j) * groups + group]
    along = jnp.sum(q_unit * grad, axis=-1, keepdims=True)
    grad_ref[...] = (grad - q_unit * along) / q_length

    many = groups * (tokens - 1)
    wait_out(qbuf.at[pl.ds(0, many + groups - 1)], send_sem.at[0])
    wait_out(st1.at[pl.ds(0, many)], send_sem.at[1])
    wait_out(gsend.at[pl.ds(0, many)], send_sem.at[3])
    if groups > 1:
        wait_out(st2.at[pl.ds(0, groups * (groups - 1))], send_sem.at[2])
        wait_out(yrecv.at[pl.ds(0, groups - 1)], send_sem.at[4])


def on_device(groups, tokens, queries, positive, queue, slot_order):
    docs, length, dim = queue.shape
    rows = docs * length
    lanes = HALF * tokens
    vmem = 63 * 2**20
    VM = pl.BlockSpec(memory_space=pltpu.VMEM)
    chunks = 8 if docs % 8 == 0 else 1
    f32, bf16 = jnp.float32, jnp.bfloat16
    DMA = pltpu.SemaphoreType.DMA
    grad, loss = pl.pallas_call(
        functools.partial(kernel, groups, tokens, docs, length, chunks, vmem),
        out_shape=(jax.ShapeDtypeStruct((ROWS, dim), f32), jax.ShapeDtypeStruct((1, 1), f32)),
        in_specs=[pl.BlockSpec(memory_space=pltpu.SMEM), VM, VM, pl.BlockSpec(memory_space=pl.ANY)],
        out_specs=(VM, VM),
        scratch_shapes=[
            pltpu.VMEM((2 * groups, rows, lanes), bf16),
            pltpu.VMEM((rows, dim), bf16),
            pltpu.VMEM((dim, rows), bf16),
            pltpu.VMEM((groups * tokens, ROWS, dim), bf16),
            pltpu.VMEM((2 * groups, docs, lanes), f32),
            pltpu.VMEM((2 * groups, docs, 128), f32),
            pltpu.VMEM((docs, 128), f32),
            pltpu.VMEM((groups * tokens, 1, 128), f32),
            pltpu.VMEM((groups * groups, 1, 128), f32),
            pltpu.VMEM((groups, 1, 128), f32),
            pltpu.VMEM((groups * tokens, ROWS, dim), bf16),
            pltpu.VMEM((groups * tokens, ROWS, dim), bf16),
            pltpu.VMEM((groups * groups, ROWS, dim), f32),
            DMA((chunks,)),
            DMA((groups,)),
            DMA((groups,)),
            DMA((groups,)),
            DMA((groups,)),
            DMA((groups,)),
            DMA,
            DMA((5,)),
        ],
        compiler_params=pltpu.CompilerParams(
            collective_id=0, has_side_effects=True, vmem_limit_bytes=vmem
        ),
    )(positive, queries.reshape(ROWS, dim), slot_order.reshape(1, docs), queue.reshape(rows, dim))
    return loss.reshape(()), grad.reshape(1, ROWS, dim)


def solution(mesh):
    groups, tokens = mesh.shape["group"], mesh.shape["queue"]
    return jax.shard_map(
        functools.partial(on_device, groups, tokens),
        mesh=mesh,
        in_specs=(
            P("queue", "group", None),
            P(),
            P(("group", "queue"), None, None),
            P(("group", "queue")),
        ),
        out_specs=(P(), P("queue", "group", None)),
        check_vma=False,
    )
```

```python
import functools

import jax
import jax.numpy as jnp
from jax import lax
from jax.experimental import pallas as pl
from jax.experimental.pallas import tpu as pltpu
from jax.sharding import PartitionSpec as P

sharpness = 0.1
softness_divisor = 0.05
epsilon = 1e-06
log2e = 1.4426950408889634
MESH = pl.DeviceIdType.MESH
ROWS = 16
HALF = 8
SUB = 8


def tile_order(u, group):
    own = lax.div(8 - u, 8)
    other = (u - 1) + lax.div(u + 7 - 2 * group, 8)
    return own * (2 * group) + (1 - own) * other


def last_order(k, group, groups):
    own = lax.div(k, groups - 1)
    other = k + lax.div(k - group + 4, 4)
    return own * group + (1 - own) * other


def kernel(
    groups, tokens, docs, length, chunks, vmem,
    pos_ref, q_ref, slot_ref, queue_ref,
    grad_ref, loss_ref,
    powered, doc, doc_t, qbuf, sums, logits, slot_col, st1, st2, fin, gsend, grecv, yrecv,
    load_sem, qy_recv, q_recv, s1_recv, s2_recv, g_recv, y_recv, send_sem,
):
    group = lax.axis_index("group")
    me = lax.axis_index("queue")
    rows = docs * length
    lanes = HALF * tokens
    chunk = rows // chunks
    blocks = 8
    block_rows = rows // blocks
    block_docs = docs // blocks

    def load(c):
        part = pl.ds(c * chunk, chunk)
        return pltpu.make_async_copy(queue_ref.at[part], doc.at[part], load_sem.at[c])

    for c in range(chunks):
        load(c).start()

    def peer_of(j):
        return lax.rem(me + j, tokens)

    def other_group(j):
        return lax.rem(group + j, groups)

    barrier = pltpu.get_barrier_semaphore()

    for j in range(1, tokens):
        pl.semaphore_signal(barrier, inc=1, device_id={"queue": peer_of(j)}, device_id_type=MESH)
    for j in range(1, groups):
        pl.semaphore_signal(barrier, inc=1, device_id={"group": other_group(j)}, device_id_type=MESH)

    wide = q_ref[...].astype(jnp.float32)
    q_length = jnp.sqrt(jnp.sum(wide * wide, axis=-1, keepdims=True) + epsilon)
    q_unit = wide / q_length
    qbuf[group * tokens + me] = q_unit.astype(jnp.bfloat16)
    slot_col[...] = jnp.broadcast_to(slot_ref[...].astype(jnp.float32), (128, docs)).T

    pl.semaphore_wait(barrier, tokens - 1 + groups - 1)

    def to_group(src, dst, send, recv, j):
        return pltpu.make_async_remote_copy(
            src_ref=src, dst_ref=dst, send_sem=send, recv_sem=recv,
            device_id={"group": j}, device_id_type=MESH,
        )

    def to_peer(src, dst, send, recv, j):
        return pltpu.make_async_remote_copy(
            src_ref=src, dst_ref=dst, send_sem=send, recv_sem=recv,
            device_id={"queue": j}, device_id_type=MESH,
        )

    def wait_in(ref, sem):
        to_peer(ref, ref, send_sem.at[0], sem, me).wait_recv()

    def wait_out(ref, sem):
        to_peer(ref, ref, sem, q_recv.at[0], me).wait_send()

    mine = qbuf.at[group * tokens + me]
    for j in range(1, groups):
        to_group(mine, mine, send_sem.at[0], qy_recv.at[group], other_group(j)).start()

    def to_all(src_of, dst, send, recv):
        for j in range(1, tokens):
            peer = peer_of(j)
            to_peer(src_of(peer), dst, send, recv, peer).start()

    def spread(g):
        block = qbuf.at[g * tokens + me]
        to_all(lambda peer: block, block, send_sem.at[0], q_recv.at[g])

    spread(group)

    def normalize(c):
        load(c).wait()
        part = pl.ds(c * chunk, chunk)
        x = doc[part, :].astype(jnp.float32)
        y = x * lax.rsqrt(jnp.sum(x * x, axis=-1, keepdims=True) + epsilon)
        y = y.reshape(chunk // (SUB * length), SUB, length, 128).swapaxes(1, 2).reshape(chunk, 128)
        doc[part, :] = y.astype(jnp.bfloat16)
        doc_t[:, part] = y.T.astype(jnp.bfloat16)

    def pass_on(j):
        g = other_group(j)
        block = qbuf.at[g * tokens + me]
        wait_in(block, qy_recv.at[g])
        spread(g)

    for c in range(chunks):
        normalize(c)
        if c == chunks // 2:
            for j in range(1, groups):
                pass_on(j)

    lane = lax.broadcasted_iota(jnp.int32, (1, 128), 1)
    spot = lax.rem(lane, HALF)
    field = lax.div(lane, HALF)

    def hits(t):
        wanted = jnp.zeros((1, 128), jnp.float32)
        for b in range(HALF):
            wanted = jnp.where(spot == b, pos_ref[t * HALF + b].astype(jnp.float32), wanted)
        return slot_col[...] == wanted

    def everywhere(x):
        for shift in (8, 16, 32, 64):
            x = x + pltpu.roll(x, shift, 1)
        return x

    def dots(t):
        g, h = lax.div(t, 2), lax.rem(t, 2)
        q = qbuf[pl.ds(g * tokens, tokens)].astype(jnp.float32)
        q = jnp.where(h == 0, q[:, :HALF], q[:, HALF:])
        q = q.reshape(lanes, 128).T.astype(jnp.bfloat16)
        for c in range(blocks):
            part = pl.ds(c * block_rows, block_rows)
            x = jnp.dot(doc[part, :], q, preferred_element_type=jnp.float32)
            e = jnp.exp2(x * (log2e / sharpness))
            powered[t, part, :] = e.astype(jnp.bfloat16)
            summed = jnp.sum(e.reshape(block_docs // SUB, length, SUB, lanes), axis=1)
            sums[t, c * block_docs:(c + 1) * block_docs, :] = summed.reshape(block_docs, lanes)

    def scores(t, valid):
        g, h = lax.div(t, 2), lax.rem(t, 2)
        score = jnp.log(sums[t]) * (sharpness / softness_divisor)
        total = score[:, :128]
        for c in range(1, lanes // 128):
            total = total + score[:, c * 128:(c + 1) * 128]
        total = everywhere(total)
        logits[t] = total
        top = jnp.max(total, axis=0, keepdims=True)
        mass = jnp.sum(jnp.exp(total - top), axis=0, keepdims=True)
        target = jnp.sum(jnp.where(hits(t), total, 0.0), axis=0, keepdims=True)
        row = jnp.where(field == h, top, 0.0)
        row = jnp.where(field == 4 + h, mass, row)
        row = jnp.where(field == 6 + h, target, row)
        at = (valid * g + (1 - valid) * (groups - 1)) * tokens + me
        st1[at] = st1[at] + jnp.where(valid > 0, row, 0.0)

    def combine(parts):
        top = jnp.max(parts, axis=0)
        shifted = pltpu.roll(parts.reshape(-1, 128), 32, 1).reshape(parts.shape)
        scale = jnp.exp(shifted - pltpu.roll(top, 32, 1)[None])
        return jnp.where(field < 4, top, jnp.sum(parts * scale, axis=0))

    def send_stats(g):
        block = st1.at[g * tokens + me]
        to_all(lambda peer: block, block, send_sem.at[1], s1_recv.at[g])

    def combine_plane(g):
        wait_in(st1.at[pl.ds(0, tokens - 1)], s1_recv.at[g])
        block = st2.at[g * groups + group]
        st2[g * groups + group] = combine(st1[pl.ds(g * tokens, tokens)])
        for j in range(1, groups):
            to_group(block, block, send_sem.at[2], s2_recv.at[g], other_group(j)).start()

    def combine_groups(g):
        wait_in(st2.at[pl.ds(0, groups - 1)], s2_recv.at[g])
        fin[g] = combine(st2[pl.ds(g * groups, groups)])

    def pass_a(u, carry):
        t = tile_order(u, group)
        before = tile_order(u - 1 + lax.div(8 - u, 8), group)

        @pl.when((u > 0) & (lax.rem(t, 2) == 0))
        def _():
            wait_in(qbuf.at[pl.ds(0, tokens - 1)], q_recv.at[lax.div(t, 2)])

        scores(before, lax.div(u + last, last + 1) * (1 - lax.div(u, last)))
        dots(t)

        @pl.when(u >= last - 1)
        def _():
            scores(t, 1)

        @pl.when((u >= 3) & (u != 4))
        def _():
            send_stats(lax.div(u - 2 + lax.div(u, last), 2))

        @pl.when(u == last - 1)
        def _():
            combine_plane(jnp.int32(0))

        return carry

    last = 2 * groups - 1
    sums[group * 2] = jnp.ones((docs, lanes), jnp.float32)
    for g in range(groups):
        st1[g * tokens + me] = jnp.zeros((1, 128), jnp.float32)
    wait_in(qbuf.at[pl.ds(0, tokens - 1)], q_recv.at[group])
    lax.fori_loop(0, last + 1, pass_a, 0)

    def weight(g, h):
        t = g * 2 + h
        row = fin[g]
        lse = row + jnp.log(pltpu.roll(row, 96, 1))
        lse = everywhere(jnp.where(field == h, lse, 0.0))
        c = (jnp.exp(logits[t] - lse) - hits(t).astype(jnp.float32)) / softness_divisor
        c = jnp.concatenate([c] * (lanes // 128), axis=1)
        return c / sums[t]

    def gradient(g, h, c):
        t = g * 2 + h
        out = jnp.zeros((128, lanes), jnp.float32)
        for b in range(blocks):
            part = pl.ds(b * block_rows, block_rows)
            w = []
            for d in range(b * block_docs, (b + 1) * block_docs, SUB):
                twice = jnp.concatenate([c[d:d + SUB]] * 2, axis=0).astype(jnp.bfloat16)
                p = powered[t, pl.ds(d * length, SUB * length), :]
                w.append((p.reshape(length // 2, 2 * SUB, lanes) * twice[None]).reshape(SUB * length, lanes))
            w = jnp.concatenate(w, axis=0)
            out = out + jnp.dot(doc_t[:, part], w, preferred_element_type=jnp.float32)
        return out.T.reshape(tokens, HALF, 128)

    def plane_sum(g):
        wait_in(grecv.at[pl.ds(0, tokens - 1)], g_recv.at[g])
        return jnp.sum(grecv[pl.ds(g * tokens, tokens)].astype(jnp.float32), axis=0)

    def pass_b(k, carry):
        g = last_order(k, group, groups)

        @pl.when(k == 0)
        def _():
            combine_plane(jnp.int32(1))

        @pl.when(k == 1 - lax.div(groups - group, groups))
        def _():
            combine_plane(jnp.int32(2))
            combine_plane(jnp.int32(3))

        combine_groups(g)
        c = [weight(g, h) for h in range(2)]
        both = jnp.concatenate([gradient(g, h, c[h]) for h in range(2)], axis=1)
        gsend[pl.ds(g * tokens, tokens)] = both.astype(jnp.bfloat16)
        grecv[g * tokens + me] = gsend[g * tokens + me]
        to_all(lambda peer: gsend.at[g * tokens + peer], grecv.at[g * tokens + me], send_sem.at[3], g_recv.at[g])

        return carry

    lax.fori_loop(0, groups, pass_b, 0)

    def hand_over(k, carry):
        g = last_order(k, group, groups)
        block = yrecv.at[group * groups + g]
        yrecv[group * groups + g] = plane_sum(g)
        to_group(block, block, send_sem.at[4], y_recv, g).start()
        return carry

    lax.fori_loop(0, groups - 1, hand_over, 0)

    loss = jnp.zeros((1, 128), jnp.float32)
    for g in range(groups):
        row = fin[g]
        loss = loss + (row + jnp.log(pltpu.roll(row, 96, 1)) - pltpu.roll(row, 80, 1))
    loss = jnp.sum(jnp.where(field < 2, loss, 0.0), axis=1, keepdims=True)
    loss_ref[...] = loss * (1.0 / (groups * ROWS))

    grad = plane_sum(group)
    if groups > 1:
        wait_in(yrecv.at[pl.ds(0, groups - 1)], y_recv)
        for j in range(1, groups):
            grad = grad + yrecv[other_group(j) * groups + group]
    along = jnp.sum(q_unit * grad, axis=-1, keepdims=True)
    grad_ref[...] = (grad - q_unit * along) / q_length

    many = groups * (tokens - 1)
    wait_out(qbuf.at[pl.ds(0, many + groups - 1)], send_sem.at[0])
    wait_out(st1.at[pl.ds(0, many)], send_sem.at[1])
    wait_out(gsend.at[pl.ds(0, many)], send_sem.at[3])
    if groups > 1:
        wait_out(st2.at[pl.ds(0, groups * (groups - 1))], send_sem.at[2])
        wait_out(yrecv.at[pl.ds(0, groups - 1)], send_sem.at[4])


def on_device(groups, tokens, queries, positive, queue, slot_order):
    docs, length, dim = queue.shape
    rows = docs * length
    lanes = HALF * tokens
    vmem = 63 * 2**20
    VM = pl.BlockSpec(memory_space=pltpu.VMEM)
    chunks = 8 if docs % 8 == 0 else 1
    f32, bf16 = jnp.float32, jnp.bfloat16
    DMA = pltpu.SemaphoreType.DMA
    grad, loss = pl.pallas_call(
        functools.partial(kernel, groups, tokens, docs, length, chunks, vmem),
        out_shape=(jax.ShapeDtypeStruct((ROWS, dim), f32), jax.ShapeDtypeStruct((1, 1), f32)),
        in_specs=[pl.BlockSpec(memory_space=pltpu.SMEM), VM, VM, pl.BlockSpec(memory_space=pl.ANY)],
        out_specs=(VM, VM),
        scratch_shapes=[
            pltpu.VMEM((2 * groups, rows, lanes), bf16),
            pltpu.VMEM((rows, dim), bf16),
            pltpu.VMEM((dim, rows), bf16),
            pltpu.VMEM((groups * tokens, ROWS, dim), bf16),
            pltpu.VMEM((2 * groups, docs, lanes), f32),
            pltpu.VMEM((2 * groups, docs, 128), f32),
            pltpu.VMEM((docs, 128), f32),
            pltpu.VMEM((groups * tokens, 1, 128), f32),
            pltpu.VMEM((groups * groups, 1, 128), f32),
            pltpu.VMEM((groups, 1, 128), f32),
            pltpu.VMEM((groups * tokens, ROWS, dim), bf16),
            pltpu.VMEM((groups * tokens, ROWS, dim), bf16),
            pltpu.VMEM((groups * groups, ROWS, dim), f32),
            DMA((chunks,)),
            DMA((groups,)),
            DMA((groups,)),
            DMA((groups,)),
            DMA((groups,)),
            DMA((groups,)),
            DMA,
            DMA((5,)),
        ],
        compiler_params=pltpu.CompilerParams(
            collective_id=0, has_side_effects=True, vmem_limit_bytes=vmem
        ),
    )(positive, queries.reshape(ROWS, dim), slot_order.reshape(1, docs), queue.reshape(rows, dim))
    return loss.reshape(()), grad.reshape(1, ROWS, dim)


def solution(mesh):
    groups, tokens = mesh.shape["group"], mesh.shape["queue"]
    return jax.shard_map(
        functools.partial(on_device, groups, tokens),
        mesh=mesh,
        in_specs=(
            P("queue", "group", None),
            P(),
            P(("group", "queue"), None, None),
            P(("group", "queue")),
        ),
        out_specs=(P(), P("queue", "group", None)),
        check_vma=False,
    )
```

```python
import functools

import jax
import jax.numpy as jnp
from jax import lax
from jax.experimental import pallas as pl
from jax.experimental.pallas import tpu as pltpu
from jax.sharding import PartitionSpec as P

sharpness = 0.1
softness_divisor = 0.05
epsilon = 1e-06
log2e = 1.4426950408889634
MESH = pl.DeviceIdType.MESH
ROWS = 16
SUB = 8


def tile_order(u, first):
    own = lax.div(8 - u, 8)
    other = (u - 1) + lax.div(u + 7 - first, 8)
    return own * first + (1 - own) * other


def last_order(k, group, groups):
    own = lax.div(k, groups - 1)
    other = k + lax.div(k - group + 4, 4)
    return own * group + (1 - own) * other


def kernel(
    groups, tokens, docs, length, chunks, vmem,
    pos_ref, q_ref, slot_ref, queue_ref,
    grad_ref, loss_ref,
    powered, doc, doc_t, qbuf, sums, logits, slot_col, stats, fin, gsend, grecv, yrecv,
    load_sem, qy_recv, q_recv, s_recv, g_recv, y_recv, send_sem,
):
    group = lax.axis_index("group")
    me = lax.axis_index("queue")
    rows = docs * length
    half = tokens // 2
    lanes = half * ROWS
    chunk = rows // chunks
    blocks = 8
    block_rows = rows // blocks
    block_docs = docs // blocks
    everyone = groups * tokens

    def load(c):
        part = pl.ds(c * chunk, chunk)
        return pltpu.make_async_copy(queue_ref.at[part], doc.at[part], load_sem.at[c])

    for c in range(chunks):
        load(c).start()

    def peer_of(j):
        return lax.rem(me + j, tokens)

    def other_group(j):
        return lax.rem(group + j, groups)

    barrier = pltpu.get_barrier_semaphore()

    for j in range(1, tokens):
        pl.semaphore_signal(barrier, inc=1, device_id={"queue": peer_of(j)}, device_id_type=MESH)
    for j in range(1, groups):
        pl.semaphore_signal(barrier, inc=1, device_id={"group": other_group(j)}, device_id_type=MESH)

    wide = q_ref[...].astype(jnp.float32)
    q_length = jnp.sqrt(jnp.sum(wide * wide, axis=-1, keepdims=True) + epsilon)
    q_unit = wide / q_length
    qbuf[group * tokens + me] = q_unit.astype(jnp.bfloat16)
    slot_col[...] = jnp.broadcast_to(slot_ref[...].astype(jnp.float32), (128, docs)).T

    pl.semaphore_wait(barrier, tokens - 1 + groups - 1)

    def to_group(src, dst, send, recv, j):
        return pltpu.make_async_remote_copy(
            src_ref=src, dst_ref=dst, send_sem=send, recv_sem=recv,
            device_id={"group": j}, device_id_type=MESH,
        )

    def to_peer(src, dst, send, recv, j):
        return pltpu.make_async_remote_copy(
            src_ref=src, dst_ref=dst, send_sem=send, recv_sem=recv,
            device_id={"queue": j}, device_id_type=MESH,
        )

    def wait_in(ref, sem):
        to_peer(ref, ref, send_sem.at[0], sem, me).wait_recv()

    def wait_out(ref, sem):
        to_peer(ref, ref, sem, q_recv.at[0], me).wait_send()

    mine = qbuf.at[group * tokens + me]
    for j in range(1, groups):
        to_group(mine, mine, send_sem.at[0], qy_recv.at[group], other_group(j)).start()

    mine_half = lax.div(me, half)
    near = [mine_half * half + lax.rem(me - mine_half * half + j, half) for j in range(1, half)]
    far = [(1 - mine_half) * half + j for j in range(half)]

    def spread(g):
        block = qbuf.at[g * tokens + me]
        for peer in near + far:
            to_peer(block, block, send_sem.at[0], q_recv.at[2 * g + mine_half], peer).start()

    spread(group)

    def normalize(c):
        load(c).wait()
        part = pl.ds(c * chunk, chunk)
        x = doc[part, :].astype(jnp.float32)
        y = x * lax.rsqrt(jnp.sum(x * x, axis=-1, keepdims=True) + epsilon)
        y = y.reshape(chunk // (SUB * length), SUB, length, 128).swapaxes(1, 2).reshape(chunk, 128)
        doc[part, :] = y.astype(jnp.bfloat16)
        doc_t[:, part] = y.T.astype(jnp.bfloat16)

    for c in range(chunks):
        normalize(c)

    for k in range(groups - 1):
        g = last_order(k, group, groups)
        wait_in(qbuf.at[g * tokens + me], qy_recv.at[g])
        spread(g)

    lane = lax.broadcasted_iota(jnp.int32, (1, 128), 1)
    spot = lax.rem(lane, ROWS)
    field = lax.div(lane, ROWS)

    def hits(g):
        wanted = jnp.zeros((1, 128), jnp.float32)
        for b in range(ROWS):
            wanted = jnp.where(spot == b, pos_ref[g * ROWS + b].astype(jnp.float32), wanted)
        return slot_col[...] == wanted

    def everywhere(x):
        for shift in (16, 32, 64):
            x = x + pltpu.roll(x, shift, 1)
        return x

    def dots(t):
        q = qbuf[pl.ds(t * half, half)].reshape(lanes, 128).T
        for c in range(blocks):
            part = pl.ds(c * block_rows, block_rows)
            x = jnp.dot(doc[part, :], q, preferred_element_type=jnp.float32)
            e = jnp.exp2(x * (log2e / sharpness))
            powered[t, part, :] = e.astype(jnp.bfloat16)
            summed = jnp.sum(e.reshape(block_docs // SUB, length, SUB, lanes), axis=1)
            sums[t, c * block_docs:(c + 1) * block_docs, :] = summed.reshape(block_docs, lanes)

    def scores(g):
        total = jnp.zeros((docs, 128), jnp.float32)
        for h in range(2):
            score = jnp.log(sums[2 * g + h])
            for c in range(lanes // 128):
                total = total + score[:, c * 128:(c + 1) * 128]
        total = everywhere(total) * (sharpness / softness_divisor)
        logits[g] = total
        top = jnp.max(total, axis=0, keepdims=True)
        mass = jnp.sum(jnp.exp(total - top), axis=0, keepdims=True)
        target = jnp.sum(jnp.where(hits(g), total, 0.0), axis=0, keepdims=True)
        row = jnp.where(field == 0, top, 0.0)
        row = jnp.where(field == 4, mass, row)
        stats[g * everyone + group * tokens + me] = jnp.where(field == 5, target, row)

    def send_stats(g):
        block = stats.at[g * everyone + group * tokens + me]
        for i in range(groups):
            for j in range(tokens):
                if i + j > 0:
                    pltpu.make_async_remote_copy(
                        src_ref=block, dst_ref=block, send_sem=send_sem.at[1], recv_sem=s_recv.at[g],
                        device_id=(other_group(i), peer_of(j)), device_id_type=MESH,
                    ).start()

    def combine(g):
        wait_in(stats.at[pl.ds(0, everyone - 1)], s_recv.at[g])
        parts = stats[pl.ds(g * everyone, everyone)].reshape(everyone, 128)
        top = jnp.max(parts, axis=0, keepdims=True)
        scale = jnp.exp(pltpu.roll(parts, 64, 1) - pltpu.roll(top, 64, 1))
        fin[g] = jnp.where(field < 4, top, jnp.sum(parts * scale, axis=0, keepdims=True))

    def pass_a(u, carry):
        t = tile_order(u, first)

        @pl.when((u > 0) & (lax.rem(t, 2) == mine_half))
        def _():
            wait_in(qbuf.at[pl.ds(0, half - 1)], q_recv.at[t])

        @pl.when((u > 0) & (lax.rem(t, 2) != mine_half))
        def _():
            wait_in(qbuf.at[pl.ds(0, half)], q_recv.at[t])

        dots(t)
        g = lax.div(u + 1, 2) - 1
        odd = lax.rem(u, 2)

        @pl.when(((odd == 1) & (g >= group)) | ((odd == 0) & (u > 0) & (g < group)))
        def _():
            scores(g)
            send_stats(g)

        return carry

    first = 2 * group + mine_half
    wait_in(qbuf.at[pl.ds(0, half - 1)], q_recv.at[first])
    lax.fori_loop(0, 2 * groups, pass_a, 0)

    def gradient(t, c):
        c = jnp.concatenate([c] * (lanes // 128), axis=1) / sums[t]
        out = jnp.zeros((128, lanes), jnp.float32)
        for b in range(blocks):
            part = pl.ds(b * block_rows, block_rows)
            w = []
            for d in range(b * block_docs, (b + 1) * block_docs, SUB):
                twice = jnp.concatenate([c[d:d + SUB]] * 2, axis=0).astype(jnp.bfloat16)
                p = powered[t, pl.ds(d * length, SUB * length), :]
                w.append((p.reshape(length // 2, 2 * SUB, lanes) * twice[None]).reshape(SUB * length, lanes))
            w = jnp.concatenate(w, axis=0)
            out = out + jnp.dot(doc_t[:, part], w, preferred_element_type=jnp.float32)
        gsend[pl.ds(t * half, half)] = out.T.reshape(half, ROWS, 128).astype(jnp.bfloat16)

    def send_grad(g, peers):
        for peer in peers:
            to_peer(
                gsend.at[g * tokens + peer], grecv.at[g * tokens + me], send_sem.at[3], g_recv.at[g], peer
            ).start()

    def plane_sum(g):
        wait_in(grecv.at[pl.ds(0, tokens - 1)], g_recv.at[g])
        return jnp.sum(grecv[pl.ds(g * tokens, tokens)].astype(jnp.float32), axis=0)

    def pass_b(k, carry):
        g = last_order(k, group, groups)

        combine(g)
        row = fin[g]
        lse = everywhere(jnp.where(field == 0, row + jnp.log(pltpu.roll(row, 64, 1)), 0.0))
        c = (jnp.exp(logits[g] - lse) - hits(g).astype(jnp.float32)) / softness_divisor
        gradient(2 * g + 1 - mine_half, c)
        send_grad(g, far)
        gradient(2 * g + mine_half, c)
        grecv[g * tokens + me] = gsend[g * tokens + me]
        send_grad(g, near)
        return carry

    lax.fori_loop(0, groups, pass_b, 0)

    def hand_over(k, carry):
        g = last_order(k, group, groups)
        block = yrecv.at[group * groups + g]
        yrecv[group * groups + g] = plane_sum(g)
        to_group(block, block, send_sem.at[4], y_recv, g).start()
        return carry

    lax.fori_loop(0, groups - 1, hand_over, 0)

    loss = jnp.zeros((1, 128), jnp.float32)
    for g in range(groups):
        row = fin[g]
        loss = loss + (row + jnp.log(pltpu.roll(row, 64, 1)) - pltpu.roll(row, 48, 1))
    loss = jnp.sum(jnp.where(field == 0, loss, 0.0), axis=1, keepdims=True)
    loss_ref[...] = loss * (1.0 / (groups * ROWS))

    grad = plane_sum(group)
    if groups > 1:
        wait_in(yrecv.at[pl.ds(0, groups - 1)], y_recv)
        for j in range(1, groups):
            grad = grad + yrecv[other_group(j) * groups + group]
    along = jnp.sum(q_unit * grad, axis=-1, keepdims=True)
    grad_ref[...] = (grad - q_unit * along) / q_length

    many = groups * (tokens - 1)
    wait_out(qbuf.at[pl.ds(0, many + groups - 1)], send_sem.at[0])
    wait_out(stats.at[pl.ds(0, groups * (everyone - 1))], send_sem.at[1])
    wait_out(gsend.at[pl.ds(0, many)], send_sem.at[3])
    if groups > 1:
        wait_out(yrecv.at[pl.ds(0, groups - 1)], send_sem.at[4])


def on_device(groups, tokens, queries, positive, queue, slot_order):
    docs, length, dim = queue.shape
    rows = docs * length
    half = tokens // 2
    lanes = half * ROWS
    vmem = 63 * 2**20
    VM = pl.BlockSpec(memory_space=pltpu.VMEM)
    chunks = 8 if docs % 8 == 0 else 1
    f32, bf16 = jnp.float32, jnp.bfloat16
    DMA = pltpu.SemaphoreType.DMA
    grad, loss = pl.pallas_call(
        functools.partial(kernel, groups, tokens, docs, length, chunks, vmem),
        out_shape=(jax.ShapeDtypeStruct((ROWS, dim), f32), jax.ShapeDtypeStruct((1, 1), f32)),
        in_specs=[pl.BlockSpec(memory_space=pltpu.SMEM), VM, VM, pl.BlockSpec(memory_space=pl.ANY)],
        out_specs=(VM, VM),
        scratch_shapes=[
            pltpu.VMEM((2 * groups, rows, lanes), bf16),
            pltpu.VMEM((rows, dim), bf16),
            pltpu.VMEM((dim, rows), bf16),
            pltpu.VMEM((groups * tokens, ROWS, dim), bf16),
            pltpu.VMEM((2 * groups, docs, lanes), f32),
            pltpu.VMEM((groups, docs, 128), f32),
            pltpu.VMEM((docs, 128), f32),
            pltpu.VMEM((groups * groups * tokens, 1, 128), f32),
            pltpu.VMEM((groups, 1, 128), f32),
            pltpu.VMEM((groups * tokens, ROWS, dim), bf16),
            pltpu.VMEM((groups * tokens, ROWS, dim), bf16),
            pltpu.VMEM((groups * groups, ROWS, dim), f32),
            DMA((chunks,)),
            DMA((groups,)),
            DMA((2 * groups,)),
            DMA((groups,)),
            DMA((groups,)),
            DMA,
            DMA((5,)),
        ],
        compiler_params=pltpu.CompilerParams(
            collective_id=0, has_side_effects=True, vmem_limit_bytes=vmem
        ),
    )(positive, queries.reshape(ROWS, dim), slot_order.reshape(1, docs), queue.reshape(rows, dim))
    return loss.reshape(()), grad.reshape(1, ROWS, dim)


def solution(mesh):
    groups, tokens = mesh.shape["group"], mesh.shape["queue"]
    return jax.shard_map(
        functools.partial(on_device, groups, tokens),
        mesh=mesh,
        in_specs=(
            P("queue", "group", None),
            P(),
            P(("group", "queue"), None, None),
            P(("group", "queue")),
        ),
        out_specs=(P(), P("queue", "group", None)),
        check_vma=False,
    )
```

```python
import functools

import jax
import jax.numpy as jnp
from jax import lax
from jax.experimental import pallas as pl
from jax.experimental.pallas import tpu as pltpu
from jax.sharding import PartitionSpec as P

sharpness = 0.1
softness_divisor = 0.05
epsilon = 1e-06
log2e = 1.4426950408889634
MESH = pl.DeviceIdType.MESH
ROWS = 16
SUB = 8


def tile_order(u, first):
    own = lax.div(8 - u, 8)
    other = (u - 1) + lax.div(u + 7 - first, 8)
    return own * first + (1 - own) * other


def last_order(k, group, groups):
    own = lax.div(k, groups - 1)
    other = k + lax.div(k - group + 4, 4)
    return own * group + (1 - own) * other


def kernel(
    groups, tokens, docs, length, chunks, vmem,
    pos_ref, q_ref, slot_ref, queue_ref,
    grad_ref, loss_ref,
    powered, doc, doc_t, qbuf, sums, logits, slot_col, stats, fin, gsend, grecv, yrecv,
    load_sem, qy_recv, q_recv, s_recv, g_recv, y_recv, send_sem,
):
    group = lax.axis_index("group")
    me = lax.axis_index("queue")
    rows = docs * length
    half = tokens // 2
    lanes = half * ROWS
    chunk = rows // chunks
    blocks = 8
    block_rows = rows // blocks
    block_docs = docs // blocks
    everyone = groups * tokens

    def load(c):
        part = pl.ds(c * chunk, chunk)
        return pltpu.make_async_copy(queue_ref.at[part], doc.at[part], load_sem.at[c])

    for c in range(chunks):
        load(c).start()

    def peer_of(j):
        return lax.rem(me + j, tokens)

    def other_group(j):
        return lax.rem(group + j, groups)

    barrier = pltpu.get_barrier_semaphore()

    for j in range(1, tokens):
        pl.semaphore_signal(barrier, inc=1, device_id={"queue": peer_of(j)}, device_id_type=MESH)
    for j in range(1, groups):
        pl.semaphore_signal(barrier, inc=1, device_id={"group": other_group(j)}, device_id_type=MESH)

    wide = q_ref[...].astype(jnp.float32)
    q_length = jnp.sqrt(jnp.sum(wide * wide, axis=-1, keepdims=True) + epsilon)
    q_unit = wide / q_length
    qbuf[group * tokens + me] = q_unit.astype(jnp.bfloat16)
    slot_col[...] = jnp.broadcast_to(slot_ref[...].astype(jnp.float32), (128, docs)).T

    pl.semaphore_wait(barrier, tokens - 1 + groups - 1)

    def to_group(src, dst, send, recv, j):
        return pltpu.make_async_remote_copy(
            src_ref=src, dst_ref=dst, send_sem=send, recv_sem=recv,
            device_id={"group": j}, device_id_type=MESH,
        )

    def to_peer(src, dst, send, recv, j):
        return pltpu.make_async_remote_copy(
            src_ref=src, dst_ref=dst, send_sem=send, recv_sem=recv,
            device_id={"queue": j}, device_id_type=MESH,
        )

    def wait_in(ref, sem):
        to_peer(ref, ref, send_sem.at[0], sem, me).wait_recv()

    def wait_out(ref, sem):
        to_peer(ref, ref, sem, q_recv.at[0], me).wait_send()

    mine = qbuf.at[group * tokens + me]
    for j in range(1, groups):
        to_group(mine, mine, send_sem.at[0], qy_recv.at[group], other_group(j)).start()

    mine_half = lax.div(me, half)
    near = [mine_half * half + lax.rem(me - mine_half * half + j, half) for j in range(1, half)]
    far = [(1 - mine_half) * half + lax.rem(me - mine_half * half + j, half) for j in range(half)]

    def spread(g):
        block = qbuf.at[g * tokens + me]
        for peer in near + far:
            to_peer(block, block, send_sem.at[0], q_recv.at[2 * g + mine_half], peer).start()

    spread(group)

    def normalize(c):
        load(c).wait()
        part = pl.ds(c * chunk, chunk)
        x = doc[part, :].astype(jnp.float32)
        y = x * lax.rsqrt(jnp.sum(x * x, axis=-1, keepdims=True) + epsilon)
        y = y.reshape(chunk // (SUB * length), SUB, length, 128).swapaxes(1, 2).reshape(chunk, 128)
        doc[part, :] = y.astype(jnp.bfloat16)
        doc_t[:, part] = y.T.astype(jnp.bfloat16)

    for c in range(chunks):
        normalize(c)

    for k in range(groups - 1):
        g = last_order(k, group, groups)
        wait_in(qbuf.at[g * tokens + me], qy_recv.at[g])
        spread(g)

    lane = lax.broadcasted_iota(jnp.int32, (1, 128), 1)
    spot = lax.rem(lane, ROWS)
    field = lax.div(lane, ROWS)

    def hits(g):
        wanted = jnp.zeros((1, 128), jnp.float32)
        for b in range(ROWS):
            wanted = jnp.where(spot == b, pos_ref[g * ROWS + b].astype(jnp.float32), wanted)
        return slot_col[...] == wanted

    def everywhere(x):
        for shift in (16, 32, 64):
            x = x + pltpu.roll(x, shift, 1)
        return x

    def dots(t):
        q = qbuf[pl.ds(t * half, half)].reshape(lanes, 128).T
        for c in range(blocks):
            part = pl.ds(c * block_rows, block_rows)
            x = jnp.dot(doc[part, :], q, preferred_element_type=jnp.float32)
            e = jnp.exp2(x * (log2e / sharpness))
            powered[t, part, :] = e.astype(jnp.bfloat16)
            summed = jnp.sum(e.reshape(block_docs // SUB, length, SUB, lanes), axis=1)
            sums[t, c * block_docs:(c + 1) * block_docs, :] = summed.reshape(block_docs, lanes)

    def scores(g):
        total = jnp.zeros((docs, 128), jnp.float32)
        for h in range(2):
            score = jnp.log(sums[2 * g + h])
            for c in range(lanes // 128):
                total = total + score[:, c * 128:(c + 1) * 128]
        total = everywhere(total) * (sharpness / softness_divisor)
        logits[g] = total
        top = jnp.max(total, axis=0, keepdims=True)
        mass = jnp.sum(jnp.exp(total - top), axis=0, keepdims=True)
        target = jnp.sum(jnp.where(hits(g), total, 0.0), axis=0, keepdims=True)
        row = jnp.where(field == 0, top, 0.0)
        row = jnp.where(field == 4, mass, row)
        stats[g * everyone + group * tokens + me] = jnp.where(field == 5, target, row)

    def send_stats(g):
        block = stats.at[g * everyone + group * tokens + me]
        for i in range(groups):
            for j in range(tokens):
                if i + j > 0:
                    pltpu.make_async_remote_copy(
                        src_ref=block, dst_ref=block, send_sem=send_sem.at[1], recv_sem=s_recv.at[g],
                        device_id=(other_group(i), peer_of(j)), device_id_type=MESH,
                    ).start()

    def combine(g):
        wait_in(stats.at[pl.ds(0, everyone - 1)], s_recv.at[g])
        parts = stats[pl.ds(g * everyone, everyone)].reshape(everyone, 128)
        top = jnp.max(parts, axis=0, keepdims=True)
        scale = jnp.exp(pltpu.roll(parts, 64, 1) - pltpu.roll(top, 64, 1))
        fin[g] = jnp.where(field < 4, top, jnp.sum(parts * scale, axis=0, keepdims=True))

    def pass_a(u, carry):
        t = tile_order(u, first)

        @pl.when((u > 0) & (lax.rem(t, 2) == mine_half))
        def _():
            wait_in(qbuf.at[pl.ds(0, half - 1)], q_recv.at[t])

        @pl.when((u > 0) & (lax.rem(t, 2) != mine_half))
        def _():
            wait_in(qbuf.at[pl.ds(0, half)], q_recv.at[t])

        dots(t)
        g = lax.div(u + 1, 2) - 1
        odd = lax.rem(u, 2)

        @pl.when(((odd == 1) & (g >= group)) | ((odd == 0) & (u > 0) & (g < group)))
        def _():
            scores(g)
            send_stats(g)

        return carry

    first = 2 * group + mine_half
    wait_in(qbuf.at[pl.ds(0, half - 1)], q_recv.at[first])
    lax.fori_loop(0, 2 * groups, pass_a, 0)

    def gradient(t, c):
        c = jnp.concatenate([c] * (lanes // 128), axis=1) / sums[t]
        out = jnp.zeros((128, lanes), jnp.float32)
        for b in range(blocks):
            part = pl.ds(b * block_rows, block_rows)
            w = []
            for d in range(b * block_docs, (b + 1) * block_docs, SUB):
                twice = jnp.concatenate([c[d:d + SUB]] * 2, axis=0).astype(jnp.bfloat16)
                p = powered[t, pl.ds(d * length, SUB * length), :]
                w.append((p.reshape(length // 2, 2 * SUB, lanes) * twice[None]).reshape(SUB * length, lanes))
            w = jnp.concatenate(w, axis=0)
            out = out + jnp.dot(doc_t[:, part], w, preferred_element_type=jnp.float32)
        gsend[pl.ds(t * half, half)] = out.T.reshape(half, ROWS, 128).astype(jnp.bfloat16)

    def send_grad(g, peers):
        for peer in peers:
            to_peer(
                gsend.at[g * tokens + peer], grecv.at[g * tokens + me], send_sem.at[3], g_recv.at[g], peer
            ).start()

    def plane_sum(g):
        wait_in(grecv.at[pl.ds(0, tokens - 1)], g_recv.at[g])
        return jnp.sum(grecv[pl.ds(g * tokens, tokens)].astype(jnp.float32), axis=0)

    def pass_b(k, carry):
        g = last_order(k, group, groups)

        combine(g)
        row = fin[g]
        lse = everywhere(jnp.where(field == 0, row + jnp.log(pltpu.roll(row, 64, 1)), 0.0))
        c = (jnp.exp(logits[g] - lse) - hits(g).astype(jnp.float32)) / softness_divisor
        gradient(2 * g + 1 - mine_half, c)
        gradient(2 * g + mine_half, c)
        grecv[g * tokens + me] = gsend[g * tokens + me]
        send_grad(g, near + far)
        return carry

    lax.fori_loop(0, groups, pass_b, 0)

    def hand_over(k, carry):
        g = last_order(k, group, groups)
        block = yrecv.at[group * groups + g]
        yrecv[group * groups + g] = plane_sum(g)
        to_group(block, block, send_sem.at[4], y_recv, g).start()
        return carry

    lax.fori_loop(0, groups - 1, hand_over, 0)

    loss = jnp.zeros((1, 128), jnp.float32)
    for g in range(groups):
        row = fin[g]
        loss = loss + (row + jnp.log(pltpu.roll(row, 64, 1)) - pltpu.roll(row, 48, 1))
    loss = jnp.sum(jnp.where(field == 0, loss, 0.0), axis=1, keepdims=True)
    loss_ref[...] = loss * (1.0 / (groups * ROWS))

    grad = plane_sum(group)
    if groups > 1:
        wait_in(yrecv.at[pl.ds(0, groups - 1)], y_recv)
        for j in range(1, groups):
            grad = grad + yrecv[other_group(j) * groups + group]
    along = jnp.sum(q_unit * grad, axis=-1, keepdims=True)
    grad_ref[...] = (grad - q_unit * along) / q_length

    many = groups * (tokens - 1)
    wait_out(qbuf.at[pl.ds(0, many + groups - 1)], send_sem.at[0])
    wait_out(stats.at[pl.ds(0, groups * (everyone - 1))], send_sem.at[1])
    wait_out(gsend.at[pl.ds(0, many)], send_sem.at[3])
    if groups > 1:
        wait_out(yrecv.at[pl.ds(0, groups - 1)], send_sem.at[4])


def on_device(groups, tokens, queries, positive, queue, slot_order):
    docs, length, dim = queue.shape
    rows = docs * length
    half = tokens // 2
    lanes = half * ROWS
    vmem = 63 * 2**20
    VM = pl.BlockSpec(memory_space=pltpu.VMEM)
    chunks = 8 if docs % 8 == 0 else 1
    f32, bf16 = jnp.float32, jnp.bfloat16
    DMA = pltpu.SemaphoreType.DMA
    grad, loss = pl.pallas_call(
        functools.partial(kernel, groups, tokens, docs, length, chunks, vmem),
        out_shape=(jax.ShapeDtypeStruct((ROWS, dim), f32), jax.ShapeDtypeStruct((1, 1), f32)),
        in_specs=[pl.BlockSpec(memory_space=pltpu.SMEM), VM, VM, pl.BlockSpec(memory_space=pl.ANY)],
        out_specs=(VM, VM),
        scratch_shapes=[
            pltpu.VMEM((2 * groups, rows, lanes), bf16),
            pltpu.VMEM((rows, dim), bf16),
            pltpu.VMEM((dim, rows), bf16),
            pltpu.VMEM((groups * tokens, ROWS, dim), bf16),
            pltpu.VMEM((2 * groups, docs, lanes), f32),
            pltpu.VMEM((groups, docs, 128), f32),
            pltpu.VMEM((docs, 128), f32),
            pltpu.VMEM((groups * groups * tokens, 1, 128), f32),
            pltpu.VMEM((groups, 1, 128), f32),
            pltpu.VMEM((groups * tokens, ROWS, dim), bf16),
            pltpu.VMEM((groups * tokens, ROWS, dim), bf16),
            pltpu.VMEM((groups * groups, ROWS, dim), f32),
            DMA((chunks,)),
            DMA((groups,)),
            DMA((2 * groups,)),
            DMA((groups,)),
            DMA((groups,)),
            DMA,
            DMA((5,)),
        ],
        compiler_params=pltpu.CompilerParams(
            collective_id=0, has_side_effects=True, vmem_limit_bytes=vmem
        ),
    )(positive, queries.reshape(ROWS, dim), slot_order.reshape(1, docs), queue.reshape(rows, dim))
    return loss.reshape(()), grad.reshape(1, ROWS, dim)


def solution(mesh):
    groups, tokens = mesh.shape["group"], mesh.shape["queue"]
    return jax.shard_map(
        functools.partial(on_device, groups, tokens),
        mesh=mesh,
        in_specs=(
            P("queue", "group", None),
            P(),
            P(("group", "queue"), None, None),
            P(("group", "queue")),
        ),
        out_specs=(P(), P("queue", "group", None)),
        check_vma=False,
    )
```

```python
import functools

import jax
import jax.numpy as jnp
from jax import lax
from jax.experimental import pallas as pl
from jax.experimental.pallas import tpu as pltpu
from jax.sharding import PartitionSpec as P

sharpness = 0.1
softness_divisor = 0.05
epsilon = 1e-06
log2e = 1.4426950408889634
MESH = pl.DeviceIdType.MESH
ROWS = 16
SUB = 8


def first_order(k, group):
    own = lax.div(4 - k, 4)
    other = (k - 1) + lax.div(k + 3 - group, 4)
    return own * group + (1 - own) * other


def last_order(k, group, groups):
    own = lax.div(k, groups - 1)
    other = k + lax.div(k - group + 4, 4)
    return own * group + (1 - own) * other


def kernel(
    groups, tokens, docs, length, chunks, vmem,
    pos_ref, q_ref, slot_ref, queue_ref,
    grad_ref, loss_ref,
    powered, doc, doc_t, qbuf, sums, logits, slot_col, stats, fin, gsend, grecv, yrecv,
    load_sem, qy_recv, q_recv, s_recv, g_recv, y_recv, send_sem,
):
    group = lax.axis_index("group")
    me = lax.axis_index("queue")
    rows = docs * length
    half = tokens // 2
    lanes = half * ROWS
    chunk = rows // chunks
    blocks = 8
    block_rows = rows // blocks
    block_docs = docs // blocks
    everyone = groups * tokens

    def load(c):
        part = pl.ds(c * chunk, chunk)
        return pltpu.make_async_copy(queue_ref.at[part], doc.at[part], load_sem.at[c])

    for c in range(chunks):
        load(c).start()

    def peer_of(j):
        return lax.rem(me + j, tokens)

    def other_group(j):
        return lax.rem(group + j, groups)

    barrier = pltpu.get_barrier_semaphore()

    for j in range(1, tokens):
        pl.semaphore_signal(barrier, inc=1, device_id={"queue": peer_of(j)}, device_id_type=MESH)
    for j in range(1, groups):
        pl.semaphore_signal(barrier, inc=1, device_id={"group": other_group(j)}, device_id_type=MESH)

    wide = q_ref[...].astype(jnp.float32)
    q_length = jnp.sqrt(jnp.sum(wide * wide, axis=-1, keepdims=True) + epsilon)
    q_unit = wide / q_length
    qbuf[group * tokens + me] = q_unit.astype(jnp.bfloat16)
    slot_col[...] = jnp.broadcast_to(slot_ref[...].astype(jnp.float32), (128, docs)).T

    pl.semaphore_wait(barrier, tokens - 1 + groups - 1)

    def to_group(src, dst, send, recv, j):
        return pltpu.make_async_remote_copy(
            src_ref=src, dst_ref=dst, send_sem=send, recv_sem=recv,
            device_id={"group": j}, device_id_type=MESH,
        )

    def to_peer(src, dst, send, recv, j):
        return pltpu.make_async_remote_copy(
            src_ref=src, dst_ref=dst, send_sem=send, recv_sem=recv,
            device_id={"queue": j}, device_id_type=MESH,
        )

    def wait_in(ref, sem):
        to_peer(ref, ref, send_sem.at[0], sem, me).wait_recv()

    def wait_out(ref, sem):
        to_peer(ref, ref, sem, q_recv.at[0], me).wait_send()

    mine = qbuf.at[group * tokens + me]
    for j in range(1, groups):
        to_group(mine, mine, send_sem.at[0], qy_recv.at[group], other_group(j)).start()

    mine_half = lax.div(me, half)
    near = [mine_half * half + lax.rem(me - mine_half * half + j, half) for j in range(1, half)]
    far = [(1 - mine_half) * half + lax.rem(me - mine_half * half + j, half) for j in range(half)]

    def spread(g):
        block = qbuf.at[g * tokens + me]
        for peer in near + far:
            to_peer(block, block, send_sem.at[0], q_recv.at[2 * g + mine_half], peer).start()

    spread(group)

    def normalize(c):
        load(c).wait()
        part = pl.ds(c * chunk, chunk)
        x = doc[part, :].astype(jnp.float32)
        y = x * lax.rsqrt(jnp.sum(x * x, axis=-1, keepdims=True) + epsilon)
        y = y.reshape(chunk // (SUB * length), SUB, length, 128).swapaxes(1, 2).reshape(chunk, 128)
        doc[part, :] = y.astype(jnp.bfloat16)
        doc_t[:, part] = y.T.astype(jnp.bfloat16)

    for c in range(chunks):
        normalize(c)

    for k in range(groups - 1):
        g = last_order(k, group, groups)
        wait_in(qbuf.at[g * tokens + me], qy_recv.at[g])
        spread(g)

    lane = lax.broadcasted_iota(jnp.int32, (1, 128), 1)
    spot = lax.rem(lane, ROWS)
    field = lax.div(lane, ROWS)

    def hits(g):
        wanted = jnp.zeros((1, 128), jnp.float32)
        for b in range(ROWS):
            wanted = jnp.where(spot == b, pos_ref[g * ROWS + b].astype(jnp.float32), wanted)
        return slot_col[...] == wanted

    def everywhere(x):
        for shift in (16, 32, 64):
            x = x + pltpu.roll(x, shift, 1)
        return x

    def dots(t):
        q = qbuf[pl.ds(t * half, half)].reshape(lanes, 128).T
        for c in range(blocks):
            part = pl.ds(c * block_rows, block_rows)
            x = jnp.dot(doc[part, :], q, preferred_element_type=jnp.float32)
            e = jnp.exp2(x * (log2e / sharpness))
            powered[t, part, :] = e.astype(jnp.bfloat16)
            summed = jnp.sum(e.reshape(block_docs // SUB, length, SUB, lanes), axis=1)
            sums[t, c * block_docs:(c + 1) * block_docs, :] = summed.reshape(block_docs, lanes)

    def scores(g):
        total = jnp.zeros((docs, 128), jnp.float32)
        for h in range(2):
            score = jnp.log(sums[2 * g + h])
            for c in range(lanes // 128):
                total = total + score[:, c * 128:(c + 1) * 128]
        total = everywhere(total) * (sharpness / softness_divisor)
        logits[g] = total
        top = jnp.max(total, axis=0, keepdims=True)
        mass = jnp.sum(jnp.exp(total - top), axis=0, keepdims=True)
        target = jnp.sum(jnp.where(hits(g), total, 0.0), axis=0, keepdims=True)
        row = jnp.where(field == 0, top, 0.0)
        row = jnp.where(field == 4, mass, row)
        stats[g * everyone + group * tokens + me] = jnp.where(field == 5, target, row)

    def send_stats(g):
        block = stats.at[g * everyone + group * tokens + me]
        for i in range(groups):
            for j in range(tokens):
                if i + j > 0:
                    pltpu.make_async_remote_copy(
                        src_ref=block, dst_ref=block, send_sem=send_sem.at[1], recv_sem=s_recv.at[g],
                        device_id=(other_group(i), peer_of(j)), device_id_type=MESH,
                    ).start()

    def combine(g):
        wait_in(stats.at[pl.ds(0, everyone - 1)], s_recv.at[g])
        parts = stats[pl.ds(g * everyone, everyone)].reshape(everyone, 128)
        top = jnp.max(parts, axis=0, keepdims=True)
        scale = jnp.exp(pltpu.roll(parts, 64, 1) - pltpu.roll(top, 64, 1))
        fin[g] = jnp.where(field < 4, top, jnp.sum(parts * scale, axis=0, keepdims=True))

    def wait_near(t):
        wait_in(qbuf.at[pl.ds(0, half - 1)], q_recv.at[t])

    def wait_far(t):
        wait_in(qbuf.at[pl.ds(0, half)], q_recv.at[t])

    def own_tile(i, carry):
        t = 2 * group + lax.rem(mine_half + i, 2)

        @pl.when(i == 0)
        def _():
            wait_near(t)

        @pl.when(i == 1)
        def _():
            wait_far(t)

        dots(t)
        return carry

    def pass_a(k, carry):
        g = first_order(k, group)
        before = first_order(k - 1, group)
        wait_near(2 * g + mine_half)
        wait_far(2 * g + 1 - mine_half)
        scores(before)
        send_stats(before)
        dots(2 * g)
        dots(2 * g + 1)
        return carry

    lax.fori_loop(0, 2, own_tile, 0)
    lax.fori_loop(1, groups, pass_a, 0)
    final = first_order(jnp.int32(groups - 1), group)
    scores(final)
    send_stats(final)

    def gradient(t, c):
        c = jnp.concatenate([c] * (lanes // 128), axis=1) / sums[t]
        out = jnp.zeros((128, lanes), jnp.float32)
        for b in range(blocks):
            part = pl.ds(b * block_rows, block_rows)
            w = []
            for d in range(b * block_docs, (b + 1) * block_docs, SUB):
                twice = jnp.concatenate([c[d:d + SUB]] * 2, axis=0).astype(jnp.bfloat16)
                p = powered[t, pl.ds(d * length, SUB * length), :]
                w.append((p.reshape(length // 2, 2 * SUB, lanes) * twice[None]).reshape(SUB * length, lanes))
            w = jnp.concatenate(w, axis=0)
            out = out + jnp.dot(doc_t[:, part], w, preferred_element_type=jnp.float32)
        gsend[pl.ds(t * half, half)] = out.T.reshape(half, ROWS, 128).astype(jnp.bfloat16)

    def send_grad(g, peers):
        for peer in peers:
            to_peer(
                gsend.at[g * tokens + peer], grecv.at[g * tokens + me], send_sem.at[3], g_recv.at[g], peer
            ).start()

    def plane_sum(g):
        wait_in(grecv.at[pl.ds(0, tokens - 1)], g_recv.at[g])
        return jnp.sum(grecv[pl.ds(g * tokens, tokens)].astype(jnp.float32), axis=0)

    rest = groups - 1 - group
    pivot = group + rest * lax.div(rest, 2)

    def pass_b(k, carry):
        g = last_order(k, pivot, groups)

        combine(g)
        row = fin[g]
        lse = everywhere(jnp.where(field == 0, row + jnp.log(pltpu.roll(row, 64, 1)), 0.0))
        c = (jnp.exp(logits[g] - lse) - hits(g).astype(jnp.float32)) / softness_divisor
        gradient(2 * g + 1 - mine_half, c)
        gradient(2 * g + mine_half, c)
        grecv[g * tokens + me] = gsend[g * tokens + me]
        send_grad(g, near + far)
        return carry

    lax.fori_loop(0, groups, pass_b, 0)

    def hand_over(k, carry):
        g = last_order(k, group, groups)
        block = yrecv.at[group * groups + g]
        yrecv[group * groups + g] = plane_sum(g)
        to_group(block, block, send_sem.at[4], y_recv, g).start()
        return carry

    lax.fori_loop(0, groups - 1, hand_over, 0)

    loss = jnp.zeros((1, 128), jnp.float32)
    for g in range(groups):
        row = fin[g]
        loss = loss + (row + jnp.log(pltpu.roll(row, 64, 1)) - pltpu.roll(row, 48, 1))
    loss = jnp.sum(jnp.where(field == 0, loss, 0.0), axis=1, keepdims=True)
    loss_ref[...] = loss * (1.0 / (groups * ROWS))

    grad = plane_sum(group)
    if groups > 1:
        wait_in(yrecv.at[pl.ds(0, groups - 1)], y_recv)
        for j in range(1, groups):
            grad = grad + yrecv[other_group(j) * groups + group]
    along = jnp.sum(q_unit * grad, axis=-1, keepdims=True)
    grad_ref[...] = (grad - q_unit * along) / q_length

    many = groups * (tokens - 1)
    wait_out(qbuf.at[pl.ds(0, many + groups - 1)], send_sem.at[0])
    wait_out(stats.at[pl.ds(0, groups * (everyone - 1))], send_sem.at[1])
    wait_out(gsend.at[pl.ds(0, many)], send_sem.at[3])
    if groups > 1:
        wait_out(yrecv.at[pl.ds(0, groups - 1)], send_sem.at[4])


def on_device(groups, tokens, queries, positive, queue, slot_order):
    docs, length, dim = queue.shape
    rows = docs * length
    half = tokens // 2
    lanes = half * ROWS
    vmem = 63 * 2**20
    VM = pl.BlockSpec(memory_space=pltpu.VMEM)
    chunks = 8 if docs % 8 == 0 else 1
    f32, bf16 = jnp.float32, jnp.bfloat16
    DMA = pltpu.SemaphoreType.DMA
    grad, loss = pl.pallas_call(
        functools.partial(kernel, groups, tokens, docs, length, chunks, vmem),
        out_shape=(jax.ShapeDtypeStruct((ROWS, dim), f32), jax.ShapeDtypeStruct((1, 1), f32)),
        in_specs=[pl.BlockSpec(memory_space=pltpu.SMEM), VM, VM, pl.BlockSpec(memory_space=pl.ANY)],
        out_specs=(VM, VM),
        scratch_shapes=[
            pltpu.VMEM((2 * groups, rows, lanes), bf16),
            pltpu.VMEM((rows, dim), bf16),
            pltpu.VMEM((dim, rows), bf16),
            pltpu.VMEM((groups * tokens, ROWS, dim), bf16),
            pltpu.VMEM((2 * groups, docs, lanes), f32),
            pltpu.VMEM((groups, docs, 128), f32),
            pltpu.VMEM((docs, 128), f32),
            pltpu.VMEM((groups * groups * tokens, 1, 128), f32),
            pltpu.VMEM((groups, 1, 128), f32),
            pltpu.VMEM((groups * tokens, ROWS, dim), bf16),
            pltpu.VMEM((groups * tokens, ROWS, dim), bf16),
            pltpu.VMEM((groups * groups, ROWS, dim), f32),
            DMA((chunks,)),
            DMA((groups,)),
            DMA((2 * groups,)),
            DMA((groups,)),
            DMA((groups,)),
            DMA,
            DMA((5,)),
        ],
        compiler_params=pltpu.CompilerParams(
            collective_id=0, has_side_effects=True, vmem_limit_bytes=vmem
        ),
    )(positive, queries.reshape(ROWS, dim), slot_order.reshape(1, docs), queue.reshape(rows, dim))
    return loss.reshape(()), grad.reshape(1, ROWS, dim)


def solution(mesh):
    groups, tokens = mesh.shape["group"], mesh.shape["queue"]
    return jax.shard_map(
        functools.partial(on_device, groups, tokens),
        mesh=mesh,
        in_specs=(
            P("queue", "group", None),
            P(),
            P(("group", "queue"), None, None),
            P(("group", "queue")),
        ),
        out_specs=(P(), P("queue", "group", None)),
        check_vma=False,
    )
```

```python
import functools

import jax
import jax.numpy as jnp
from jax import lax
from jax.experimental import pallas as pl
from jax.experimental.pallas import tpu as pltpu
from jax.sharding import PartitionSpec as P

sharpness = 0.1
softness_divisor = 0.05
epsilon = 1e-06
log2e = 1.4426950408889634
MESH = pl.DeviceIdType.MESH
ROWS = 16
SUB = 8


def first_order(k, group):
    own = lax.div(4 - k, 4)
    other = (k - 1) + lax.div(k + 3 - group, 4)
    return own * group + (1 - own) * other


def last_order(k, group, groups):
    own = lax.div(k, groups - 1)
    other = k + lax.div(k - group + 4, 4)
    return own * group + (1 - own) * other


def kernel(
    groups, tokens, docs, length, chunks, vmem,
    pos_in, q_in, slot_in, queue_ref,
    grad_ref, loss_ref,
    pos_ref, q_ref, slot_ref, powered, doc, doc_t, qbuf, sums, logits, slot_col, stats, fin, gsend, grecv, yrecv,
    small_sem, load_sem, qy_recv, q_recv, s_recv, g_recv, y_recv, send_sem,
):
    group = lax.axis_index("group")
    me = lax.axis_index("queue")
    rows = docs * length
    half = tokens // 2
    lanes = half * ROWS
    chunk = rows // chunks
    blocks = 8
    block_rows = rows // blocks
    block_docs = docs // blocks
    everyone = groups * tokens

    def load(c):
        part = pl.ds(c * chunk, chunk)
        return pltpu.make_async_copy(queue_ref.at[part], doc.at[part], load_sem.at[c])

    small = [
        pltpu.make_async_copy(src, dst, small_sem.at[n])
        for n, (src, dst) in enumerate(((q_in, q_ref), (slot_in, slot_ref), (pos_in, pos_ref)))
    ]
    for copy in small:
        copy.start()

    def peer_of(j):
        return lax.rem(me + j, tokens)

    def other_group(j):
        return lax.rem(group + j, groups)

    barrier = pltpu.get_barrier_semaphore()

    def hops(j):
        x, z = j % 8 // 2, j // 8 % 4
        return min(x, 4 - x) + min(z, 4 - z)

    around = sorted(range(1, tokens), key=hops, reverse=True)
    for j in around:
        pl.semaphore_signal(barrier, inc=1, device_id={"queue": peer_of(j)}, device_id_type=MESH)
    for j in range(1, groups):
        pl.semaphore_signal(barrier, inc=1, device_id={"group": other_group(j)}, device_id_type=MESH)
    for c in range(chunks):
        load(c).start()
    for copy in small:
        copy.wait()

    wide = q_ref[...].astype(jnp.float32)
    q_length = jnp.sqrt(jnp.sum(wide * wide, axis=-1, keepdims=True) + epsilon)
    q_unit = wide / q_length
    qbuf[group * tokens + me] = q_unit.astype(jnp.bfloat16)
    slot_col[...] = jnp.broadcast_to(slot_ref[...].astype(jnp.float32), (128, docs)).T

    pl.semaphore_wait(barrier, tokens - 1 + groups - 1)

    def to_group(src, dst, send, recv, j):
        return pltpu.make_async_remote_copy(
            src_ref=src, dst_ref=dst, send_sem=send, recv_sem=recv,
            device_id={"group": j}, device_id_type=MESH,
        )

    def to_peer(src, dst, send, recv, j):
        return pltpu.make_async_remote_copy(
            src_ref=src, dst_ref=dst, send_sem=send, recv_sem=recv,
            device_id={"queue": j}, device_id_type=MESH,
        )

    def wait_in(ref, sem):
        to_peer(ref, ref, send_sem.at[0], sem, me).wait_recv()

    def wait_out(ref, sem):
        to_peer(ref, ref, sem, q_recv.at[0], me).wait_send()

    mine = qbuf.at[group * tokens + me]
    for j in range(1, groups):
        to_group(mine, mine, send_sem.at[0], qy_recv.at[group], other_group(j)).start()

    mine_half = lax.div(me, half)
    near = [mine_half * half + lax.rem(me - mine_half * half + j, half) for j in sorted(range(1, half), key=hops, reverse=True)]
    far = [(1 - mine_half) * half + lax.rem(me - mine_half * half + j, half) for j in range(half)]

    def spread(g):
        block = qbuf.at[g * tokens + me]
        for peer in near + far:
            to_peer(block, block, send_sem.at[0], q_recv.at[2 * g + mine_half], peer).start()

    spread(group)

    def normalize(c):
        load(c).wait()
        part = pl.ds(c * chunk, chunk)
        x = doc[part, :].astype(jnp.float32)
        y = x * lax.rsqrt(jnp.sum(x * x, axis=-1, keepdims=True) + epsilon)
        y = y.reshape(chunk // (SUB * length), SUB, length, 128).swapaxes(1, 2).reshape(chunk, 128)
        doc[part, :] = y.astype(jnp.bfloat16)
        doc_t[:, part] = y.T.astype(jnp.bfloat16)

    for c in range(chunks):
        normalize(c)

    for k in range(groups - 1):
        g = last_order(k, group, groups)
        wait_in(qbuf.at[g * tokens + me], qy_recv.at[g])
        spread(g)

    lane = lax.broadcasted_iota(jnp.int32, (1, 128), 1)
    spot = lax.rem(lane, ROWS)
    field = lax.div(lane, ROWS)

    def hits(g):
        wanted = jnp.zeros((1, 128), jnp.float32)
        for b in range(ROWS):
            wanted = jnp.where(spot == b, pos_ref[g * ROWS + b].astype(jnp.float32), wanted)
        return slot_col[...] == wanted

    def everywhere(x):
        for shift in (16, 32, 64):
            x = x + pltpu.roll(x, shift, 1)
        return x

    def dots(t):
        q = qbuf[pl.ds(t * half, half)].reshape(lanes, 128).T
        for c in range(blocks):
            part = pl.ds(c * block_rows, block_rows)
            x = jnp.dot(doc[part, :], q, preferred_element_type=jnp.float32)
            e = jnp.exp2(x * (log2e / sharpness))
            powered[t, part, :] = e.astype(jnp.bfloat16)
            summed = jnp.sum(e.reshape(block_docs // SUB, length, SUB, lanes), axis=1)
            sums[t, c * block_docs:(c + 1) * block_docs, :] = summed.reshape(block_docs, lanes)

    def scores(g):
        total = jnp.zeros((docs, 128), jnp.float32)
        for h in range(2):
            score = jnp.log(sums[2 * g + h])
            for c in range(lanes // 128):
                total = total + score[:, c * 128:(c + 1) * 128]
        total = everywhere(total) * (sharpness / softness_divisor)
        logits[g] = total
        top = jnp.max(total, axis=0, keepdims=True)
        mass = jnp.sum(jnp.exp(total - top), axis=0, keepdims=True)
        target = jnp.sum(jnp.where(hits(g), total, 0.0), axis=0, keepdims=True)
        row = jnp.where(field == 0, top, 0.0)
        row = jnp.where(field == 4, mass, row)
        stats[g * everyone + group * tokens + me] = jnp.where(field == 5, target, row)

    def send_stats(g):
        block = stats.at[g * everyone + group * tokens + me]
        steps = [(i, j) for i in range(groups) for j in range(tokens) if i + j > 0]
        for i, j in sorted(steps, key=lambda s: hops(s[1]) + min(s[0], groups - s[0]), reverse=True):
            pltpu.make_async_remote_copy(
                src_ref=block, dst_ref=block, send_sem=send_sem.at[1], recv_sem=s_recv.at[g],
                device_id=(other_group(i), peer_of(j)), device_id_type=MESH,
            ).start()

    def combine(g):
        wait_in(stats.at[pl.ds(0, everyone - 1)], s_recv.at[g])
        parts = stats[pl.ds(g * everyone, everyone)].reshape(everyone, 128)
        top = jnp.max(parts, axis=0, keepdims=True)
        scale = jnp.exp(pltpu.roll(parts, 64, 1) - pltpu.roll(top, 64, 1))
        fin[g] = jnp.where(field < 4, top, jnp.sum(parts * scale, axis=0, keepdims=True))

    def wait_near(t):
        wait_in(qbuf.at[pl.ds(0, half - 1)], q_recv.at[t])

    def wait_far(t):
        wait_in(qbuf.at[pl.ds(0, half)], q_recv.at[t])

    def own_tile(i, carry):
        t = 2 * group + lax.rem(mine_half + i, 2)

        @pl.when(i == 0)
        def _():
            wait_near(t)

        @pl.when(i == 1)
        def _():
            wait_far(t)

        dots(t)
        return carry

    def pass_a(k, carry):
        g = first_order(k, group)
        before = first_order(k - 1, group)
        wait_near(2 * g + mine_half)
        wait_far(2 * g + 1 - mine_half)
        scores(before)
        send_stats(before)
        dots(2 * g)
        dots(2 * g + 1)
        return carry

    lax.fori_loop(0, 2, own_tile, 0)
    lax.fori_loop(1, groups, pass_a, 0)
    final = first_order(jnp.int32(groups - 1), group)
    scores(final)
    send_stats(final)

    def gradient(t, c):
        c = jnp.concatenate([c] * (lanes // 128), axis=1) / sums[t]
        out = jnp.zeros((128, lanes), jnp.float32)
        for b in range(blocks):
            part = pl.ds(b * block_rows, block_rows)
            w = []
            for d in range(b * block_docs, (b + 1) * block_docs, SUB):
                twice = jnp.concatenate([c[d:d + SUB]] * 2, axis=0).astype(jnp.bfloat16)
                p = powered[t, pl.ds(d * length, SUB * length), :]
                w.append((p.reshape(length // 2, 2 * SUB, lanes) * twice[None]).reshape(SUB * length, lanes))
            w = jnp.concatenate(w, axis=0)
            out = out + jnp.dot(doc_t[:, part], w, preferred_element_type=jnp.float32)
        gsend[pl.ds(t * half, half)] = out.T.reshape(half, ROWS, 128).astype(jnp.bfloat16)

    def send_grad(g, peers):
        for peer in peers:
            to_peer(
                gsend.at[g * tokens + peer], grecv.at[g * tokens + me], send_sem.at[3], g_recv.at[g], peer
            ).start()

    def plane_sum(g):
        wait_in(grecv.at[pl.ds(0, tokens - 1)], g_recv.at[g])
        return jnp.sum(grecv[pl.ds(g * tokens, tokens)].astype(jnp.float32), axis=0)

    rest = groups - 1 - group
    pivot = group + rest * lax.div(rest, 2)

    def pass_b(k, carry):
        g = last_order(k, pivot, groups)

        combine(g)
        row = fin[g]
        lse = everywhere(jnp.where(field == 0, row + jnp.log(pltpu.roll(row, 64, 1)), 0.0))
        c = (jnp.exp(logits[g] - lse) - hits(g).astype(jnp.float32)) / softness_divisor
        gradient(2 * g + 1 - mine_half, c)
        gradient(2 * g + mine_half, c)
        grecv[g * tokens + me] = gsend[g * tokens + me]
        send_grad(g, far + near)
        return carry

    lax.fori_loop(0, groups, pass_b, 0)

    def hand_over(k, carry):
        g = last_order(k, group, groups)
        block = yrecv.at[group * groups + g]
        yrecv[group * groups + g] = plane_sum(g)
        to_group(block, block, send_sem.at[4], y_recv, g).start()
        return carry

    lax.fori_loop(0, groups - 1, hand_over, 0)

    loss = jnp.zeros((1, 128), jnp.float32)
    for g in range(groups):
        row = fin[g]
        loss = loss + (row + jnp.log(pltpu.roll(row, 64, 1)) - pltpu.roll(row, 48, 1))
    loss = jnp.sum(jnp.where(field == 0, loss, 0.0), axis=1, keepdims=True)
    loss_ref[...] = loss * (1.0 / (groups * ROWS))

    grad = plane_sum(group)
    if groups > 1:
        wait_in(yrecv.at[pl.ds(0, groups - 1)], y_recv)
        for j in range(1, groups):
            grad = grad + yrecv[other_group(j) * groups + group]
    along = jnp.sum(q_unit * grad, axis=-1, keepdims=True)
    grad_ref[...] = (grad - q_unit * along) / q_length

    many = groups * (tokens - 1)
    wait_out(qbuf.at[pl.ds(0, many + groups - 1)], send_sem.at[0])
    wait_out(stats.at[pl.ds(0, groups * (everyone - 1))], send_sem.at[1])
    wait_out(gsend.at[pl.ds(0, many)], send_sem.at[3])
    if groups > 1:
        wait_out(yrecv.at[pl.ds(0, groups - 1)], send_sem.at[4])


def on_device(groups, tokens, queries, positive, queue, slot_order):
    docs, length, dim = queue.shape
    rows = docs * length
    half = tokens // 2
    lanes = half * ROWS
    vmem = 63 * 2**20
    VM = pl.BlockSpec(memory_space=pltpu.VMEM)
    chunks = 8 if docs % 8 == 0 else 1
    f32, bf16 = jnp.float32, jnp.bfloat16
    DMA = pltpu.SemaphoreType.DMA
    grad, loss = pl.pallas_call(
        functools.partial(kernel, groups, tokens, docs, length, chunks, vmem),
        out_shape=(jax.ShapeDtypeStruct((ROWS, dim), f32), jax.ShapeDtypeStruct((1, 1), f32)),
        in_specs=[pl.BlockSpec(memory_space=pl.ANY)] * 4,
        out_specs=(VM, VM),
        scratch_shapes=[
            pltpu.SMEM((groups * ROWS,), jnp.int32),
            pltpu.VMEM((ROWS, dim), bf16),
            pltpu.VMEM((1, docs), jnp.int32),
            pltpu.VMEM((2 * groups, rows, lanes), bf16),
            pltpu.VMEM((rows, dim), bf16),
            pltpu.VMEM((dim, rows), bf16),
            pltpu.VMEM((groups * tokens, ROWS, dim), bf16),
            pltpu.VMEM((2 * groups, docs, lanes), f32),
            pltpu.VMEM((groups, docs, 128), f32),
            pltpu.VMEM((docs, 128), f32),
            pltpu.VMEM((groups * groups * tokens, 1, 128), f32),
            pltpu.VMEM((groups, 1, 128), f32),
            pltpu.VMEM((groups * tokens, ROWS, dim), bf16),
            pltpu.VMEM((groups * tokens, ROWS, dim), bf16),
            pltpu.VMEM((groups * groups, ROWS, dim), f32),
            DMA((3,)),
            DMA((chunks,)),
            DMA((groups,)),
            DMA((2 * groups,)),
            DMA((groups,)),
            DMA((groups,)),
            DMA,
            DMA((5,)),
        ],
        compiler_params=pltpu.CompilerParams(
            collective_id=0, has_side_effects=True, vmem_limit_bytes=vmem
        ),
    )(positive, queries.reshape(ROWS, dim), slot_order.reshape(1, docs), queue.reshape(rows, dim))
    return loss.reshape(()), grad.reshape(1, ROWS, dim)


def solution(mesh):
    groups, tokens = mesh.shape["group"], mesh.shape["queue"]
    return jax.shard_map(
        functools.partial(on_device, groups, tokens),
        mesh=mesh,
        in_specs=(
            P("queue", "group", None),
            P(),
            P(("group", "queue"), None, None),
            P(("group", "queue")),
        ),
        out_specs=(P(), P("queue", "group", None)),
        check_vma=False,
    )
```

```python
import functools

import jax
import jax.numpy as jnp
from jax import lax
from jax.experimental import pallas as pl
from jax.experimental.pallas import tpu as pltpu
from jax.sharding import PartitionSpec as P

sharpness = 0.1
softness_divisor = 0.05
epsilon = 1e-06
log2e = 1.4426950408889634
MESH = pl.DeviceIdType.MESH
ROWS = 16
SUB = 8


def first_order(k, group):
    own = lax.div(4 - k, 4)
    other = (k - 1) + lax.div(k + 3 - group, 4)
    return own * group + (1 - own) * other


def last_order(k, group, groups):
    own = lax.div(k, groups - 1)
    other = k + lax.div(k - group + 4, 4)
    return own * group + (1 - own) * other


def kernel(
    groups, tokens, docs, length, chunks, vmem,
    pos_in, q_in, slot_in, queue_ref,
    grad_ref, loss_ref,
    pos_ref, q_ref, slot_ref, powered, doc, doc_t, qbuf, sums, logits, slot_col, st1, st2, stats, fin, gsend, grecv, yrecv,
    small_sem, load_sem, qy_recv, q_recv, s1_recv, s2_recv, s_recv, g_recv, y_recv, send_sem,
):
    group = lax.axis_index("group")
    me = lax.axis_index("queue")
    rows = docs * length
    half = tokens // 2
    lanes = half * ROWS
    chunk = rows // chunks
    blocks = 8
    block_rows = rows // blocks
    block_docs = docs // blocks
    everyone = groups * tokens
    early = groups - 2
    few = 2 * groups
    chips = tokens // 2
    core = lax.rem(me, 2)

    def load(c):
        part = pl.ds(c * chunk, chunk)
        return pltpu.make_async_copy(queue_ref.at[part], doc.at[part], load_sem.at[c])

    small = [
        pltpu.make_async_copy(src, dst, small_sem.at[n])
        for n, (src, dst) in enumerate(((q_in, q_ref), (slot_in, slot_ref), (pos_in, pos_ref)))
    ]
    for copy in small:
        copy.start()

    def peer_of(j):
        return lax.rem(me + j, tokens)

    def other_group(j):
        return lax.rem(group + j, groups)

    barrier = pltpu.get_barrier_semaphore()

    def hops(j):
        x, z = j % 8 // 2, j // 8 % 4
        return min(x, 4 - x) + min(z, 4 - z)

    around = sorted(range(1, tokens), key=hops, reverse=True)
    for j in around:
        pl.semaphore_signal(barrier, inc=1, device_id={"queue": peer_of(j)}, device_id_type=MESH)
    for j in range(1, groups):
        pl.semaphore_signal(barrier, inc=1, device_id={"group": other_group(j)}, device_id_type=MESH)
    for c in range(chunks):
        load(c).start()
    for copy in small:
        copy.wait()

    wide = q_ref[...].astype(jnp.float32)
    q_length = jnp.sqrt(jnp.sum(wide * wide, axis=-1, keepdims=True) + epsilon)
    q_unit = wide / q_length
    qbuf[group * tokens + me] = q_unit.astype(jnp.bfloat16)
    slot_col[...] = jnp.broadcast_to(slot_ref[...].astype(jnp.float32), (128, docs)).T

    pl.semaphore_wait(barrier, tokens - 1 + groups - 1)

    def to_group(src, dst, send, recv, j):
        return pltpu.make_async_remote_copy(
            src_ref=src, dst_ref=dst, send_sem=send, recv_sem=recv,
            device_id={"group": j}, device_id_type=MESH,
        )

    def to_peer(src, dst, send, recv, j):
        return pltpu.make_async_remote_copy(
            src_ref=src, dst_ref=dst, send_sem=send, recv_sem=recv,
            device_id={"queue": j}, device_id_type=MESH,
        )

    def wait_in(ref, sem):
        to_peer(ref, ref, send_sem.at[0], sem, me).wait_recv()

    def wait_out(ref, sem):
        to_peer(ref, ref, sem, q_recv.at[0], me).wait_send()

    mine = qbuf.at[group * tokens + me]
    for j in range(1, groups):
        to_group(mine, mine, send_sem.at[0], qy_recv.at[group], other_group(j)).start()

    mine_half = lax.div(me, half)
    near = [mine_half * half + lax.rem(me - mine_half * half + j, half) for j in sorted(range(1, half), key=hops, reverse=True)]
    far = [(1 - mine_half) * half + lax.rem(me - mine_half * half + j, half) for j in range(half)]

    def spread(g):
        block = qbuf.at[g * tokens + me]
        for peer in near + far:
            to_peer(block, block, send_sem.at[0], q_recv.at[2 * g + mine_half], peer).start()

    spread(group)

    def normalize(c):
        load(c).wait()
        part = pl.ds(c * chunk, chunk)
        x = doc[part, :].astype(jnp.float32)
        y = x * lax.rsqrt(jnp.sum(x * x, axis=-1, keepdims=True) + epsilon)
        y = y.reshape(chunk // (SUB * length), SUB, length, 128).swapaxes(1, 2).reshape(chunk, 128)
        doc[part, :] = y.astype(jnp.bfloat16)
        doc_t[:, part] = y.T.astype(jnp.bfloat16)

    for c in range(chunks):
        normalize(c)

    for k in range(groups - 1):
        g = last_order(k, group, groups)
        wait_in(qbuf.at[g * tokens + me], qy_recv.at[g])
        spread(g)

    lane = lax.broadcasted_iota(jnp.int32, (1, 128), 1)
    spot = lax.rem(lane, ROWS)
    field = lax.div(lane, ROWS)

    def hits(g):
        wanted = jnp.zeros((1, 128), jnp.float32)
        for b in range(ROWS):
            wanted = jnp.where(spot == b, pos_ref[g * ROWS + b].astype(jnp.float32), wanted)
        return slot_col[...] == wanted

    def everywhere(x):
        for shift in (16, 32, 64):
            x = x + pltpu.roll(x, shift, 1)
        return x

    def dots(t):
        q = qbuf[pl.ds(t * half, half)].reshape(lanes, 128).T
        for c in range(blocks):
            part = pl.ds(c * block_rows, block_rows)
            x = jnp.dot(doc[part, :], q, preferred_element_type=jnp.float32)
            e = jnp.exp2(x * (log2e / sharpness))
            powered[t, part, :] = e.astype(jnp.bfloat16)
            summed = jnp.sum(e.reshape(block_docs // SUB, length, SUB, lanes), axis=1)
            sums[t, c * block_docs:(c + 1) * block_docs, :] = summed.reshape(block_docs, lanes)

    def scores(g):
        total = jnp.zeros((docs, 128), jnp.float32)
        for h in range(2):
            score = jnp.log(sums[2 * g + h])
            for c in range(lanes // 128):
                total = total + score[:, c * 128:(c + 1) * 128]
        total = everywhere(total) * (sharpness / softness_divisor)
        logits[g] = total
        top = jnp.max(total, axis=0, keepdims=True)
        mass = jnp.sum(jnp.exp(total - top), axis=0, keepdims=True)
        target = jnp.sum(jnp.where(hits(g), total, 0.0), axis=0, keepdims=True)
        row = jnp.where(field == 0, top, 0.0)
        row = jnp.where(field == 4, mass, row)
        st1[g * few + group * 2 + core] = jnp.where(field == 5, target, row)

    def send_stats(g):
        block = st1.at[g * few + group * 2 + core]
        for i in range(groups):
            for j in range(2):
                if i + j > 0:
                    pltpu.make_async_remote_copy(
                        src_ref=block, dst_ref=block, send_sem=send_sem.at[1], recv_sem=s1_recv.at[g],
                        device_id=(other_group(i), me + j * (1 - 2 * core)), device_id_type=MESH,
                    ).start()

    def combine(parts):
        parts = parts.reshape(parts.shape[0], 128)
        top = jnp.max(parts, axis=0, keepdims=True)
        scale = jnp.exp(pltpu.roll(parts, 64, 1) - pltpu.roll(top, 64, 1))
        return jnp.where(field < 4, top, jnp.sum(parts * scale, axis=0, keepdims=True))

    def combine_column(g):
        wait_in(st1.at[pl.ds(0, few - 1)], s1_recv.at[g])
        row = g * chips + lax.div(me, 2)
        st2[row] = combine(st1[pl.ds(g * few, few)])
        block = st2.at[row]
        for j in range(1, chips):
            to_peer(block, block, send_sem.at[2], s2_recv.at[g], peer_of(2 * j)).start()

    def combine_plane(g):
        wait_in(st2.at[pl.ds(0, chips - 1)], s2_recv.at[g])
        fin[g] = combine(st2[pl.ds(g * chips, chips)])

    def send_all(g):
        row = (g - early) * everyone + group * tokens + me
        stats[row] = st1[g * few + group * 2 + core]
        block = stats.at[row]
        steps = [(i, j) for i in range(groups) for j in range(tokens) if i + j > 0]
        for i, j in sorted(steps, key=lambda s: hops(s[1]) + min(s[0], groups - s[0]), reverse=True):
            pltpu.make_async_remote_copy(
                src_ref=block, dst_ref=block, send_sem=send_sem.at[5], recv_sem=s_recv.at[g - early],
                device_id=(other_group(i), peer_of(j)), device_id_type=MESH,
            ).start()

    def combine_all(g):
        wait_in(stats.at[pl.ds(0, everyone - 1)], s_recv.at[g - early])
        fin[g] = combine(stats[pl.ds((g - early) * everyone, everyone)])

    def wait_near(t):
        wait_in(qbuf.at[pl.ds(0, half - 1)], q_recv.at[t])

    def wait_far(t):
        wait_in(qbuf.at[pl.ds(0, half)], q_recv.at[t])

    def own_tile(i, carry):
        t = 2 * group + lax.rem(mine_half + i, 2)

        @pl.when(i == 0)
        def _():
            wait_near(t)

        @pl.when(i == 1)
        def _():
            wait_far(t)

        dots(t)
        return carry

    def pass_a(k, carry):
        g = first_order(k, group)
        before = first_order(k - 1, group)
        wait_near(2 * g + mine_half)
        wait_far(2 * g + 1 - mine_half)
        scores(before)
        send_stats(before)
        dots(2 * g)
        dots(2 * g + 1)

        @pl.when(k == groups - 2)
        def _():
            combine_column(jnp.int32(0))

        return carry

    lax.fori_loop(0, 2, own_tile, 0)
    lax.fori_loop(1, groups, pass_a, 0)
    final = first_order(jnp.int32(groups - 1), group)
    scores(final)
    send_stats(final)
    combine_column(jnp.int32(1))
    send_all(early)
    send_all(early + 1)

    def gradient(t, c):
        c = jnp.concatenate([c] * (lanes // 128), axis=1) / sums[t]
        out = jnp.zeros((128, lanes), jnp.float32)
        for b in range(blocks):
            part = pl.ds(b * block_rows, block_rows)
            w = []
            for d in range(b * block_docs, (b + 1) * block_docs, SUB):
                twice = jnp.concatenate([c[d:d + SUB]] * 2, axis=0).astype(jnp.bfloat16)
                p = powered[t, pl.ds(d * length, SUB * length), :]
                w.append((p.reshape(length // 2, 2 * SUB, lanes) * twice[None]).reshape(SUB * length, lanes))
            w = jnp.concatenate(w, axis=0)
            out = out + jnp.dot(doc_t[:, part], w, preferred_element_type=jnp.float32)
        gsend[pl.ds(t * half, half)] = out.T.reshape(half, ROWS, 128).astype(jnp.bfloat16)

    def send_grad(g, peers):
        for peer in peers:
            to_peer(
                gsend.at[g * tokens + peer], grecv.at[g * tokens + me], send_sem.at[3], g_recv.at[g], peer
            ).start()

    def plane_sum(g):
        wait_in(grecv.at[pl.ds(0, tokens - 1)], g_recv.at[g])
        return jnp.sum(grecv[pl.ds(g * tokens, tokens)].astype(jnp.float32), axis=0)

    rest = groups - 1 - group
    pivot = group + rest * lax.div(rest, 2)

    def pass_b(k, carry):
        g = last_order(k, pivot, groups)


        @pl.when(g < early)
        def _():
            combine_plane(g)

        @pl.when(g >= early)
        def _():
            combine_all(g)

        row = fin[g]
        lse = everywhere(jnp.where(field == 0, row + jnp.log(pltpu.roll(row, 64, 1)), 0.0))
        c = (jnp.exp(logits[g] - lse) - hits(g).astype(jnp.float32)) / softness_divisor
        gradient(2 * g + 1 - mine_half, c)
        gradient(2 * g + mine_half, c)
        grecv[g * tokens + me] = gsend[g * tokens + me]
        send_grad(g, far + near)
        return carry

    lax.fori_loop(0, groups, pass_b, 0)

    def hand_over(k, carry):
        g = last_order(k, group, groups)
        block = yrecv.at[group * groups + g]
        yrecv[group * groups + g] = plane_sum(g)
        to_group(block, block, send_sem.at[4], y_recv, g).start()
        return carry

    lax.fori_loop(0, groups - 1, hand_over, 0)

    loss = jnp.zeros((1, 128), jnp.float32)
    for g in range(groups):
        row = fin[g]
        loss = loss + (row + jnp.log(pltpu.roll(row, 64, 1)) - pltpu.roll(row, 48, 1))
    loss = jnp.sum(jnp.where(field == 0, loss, 0.0), axis=1, keepdims=True)
    loss_ref[...] = loss * (1.0 / (groups * ROWS))

    grad = plane_sum(group)
    if groups > 1:
        wait_in(yrecv.at[pl.ds(0, groups - 1)], y_recv)
        for j in range(1, groups):
            grad = grad + yrecv[other_group(j) * groups + group]
    along = jnp.sum(q_unit * grad, axis=-1, keepdims=True)
    grad_ref[...] = (grad - q_unit * along) / q_length

    for g in range(early, groups):
        wait_in(st1.at[pl.ds(0, few - 1)], s1_recv.at[g])
    many = groups * (tokens - 1)
    wait_out(qbuf.at[pl.ds(0, many + groups - 1)], send_sem.at[0])
    wait_out(st1.at[pl.ds(0, groups * (few - 1))], send_sem.at[1])
    wait_out(st2.at[pl.ds(0, early * (chips - 1))], send_sem.at[2])
    wait_out(stats.at[pl.ds(0, 2 * (everyone - 1))], send_sem.at[5])
    wait_out(gsend.at[pl.ds(0, many)], send_sem.at[3])
    if groups > 1:
        wait_out(yrecv.at[pl.ds(0, groups - 1)], send_sem.at[4])


def on_device(groups, tokens, queries, positive, queue, slot_order):
    docs, length, dim = queue.shape
    rows = docs * length
    half = tokens // 2
    lanes = half * ROWS
    vmem = 63 * 2**20
    VM = pl.BlockSpec(memory_space=pltpu.VMEM)
    chunks = 8 if docs % 8 == 0 else 1
    f32, bf16 = jnp.float32, jnp.bfloat16
    DMA = pltpu.SemaphoreType.DMA
    grad, loss = pl.pallas_call(
        functools.partial(kernel, groups, tokens, docs, length, chunks, vmem),
        out_shape=(jax.ShapeDtypeStruct((ROWS, dim), f32), jax.ShapeDtypeStruct((1, 1), f32)),
        in_specs=[pl.BlockSpec(memory_space=pl.ANY)] * 4,
        out_specs=(VM, VM),
        scratch_shapes=[
            pltpu.SMEM((groups * ROWS,), jnp.int32),
            pltpu.VMEM((ROWS, dim), bf16),
            pltpu.VMEM((1, docs), jnp.int32),
            pltpu.VMEM((2 * groups, rows, lanes), bf16),
            pltpu.VMEM((rows, dim), bf16),
            pltpu.VMEM((dim, rows), bf16),
            pltpu.VMEM((groups * tokens, ROWS, dim), bf16),
            pltpu.VMEM((2 * groups, docs, lanes), f32),
            pltpu.VMEM((groups, docs, 128), f32),
            pltpu.VMEM((docs, 128), f32),
            pltpu.VMEM((groups * groups * 2, 1, 128), f32),
            pltpu.VMEM((groups * (tokens // 2), 1, 128), f32),
            pltpu.VMEM((2 * groups * tokens, 1, 128), f32),
            pltpu.VMEM((groups, 1, 128), f32),
            pltpu.VMEM((groups * tokens, ROWS, dim), bf16),
            pltpu.VMEM((groups * tokens, ROWS, dim), bf16),
            pltpu.VMEM((groups * groups, ROWS, dim), f32),
            DMA((3,)),
            DMA((chunks,)),
            DMA((groups,)),
            DMA((2 * groups,)),
            DMA((groups,)),
            DMA((groups,)),
            DMA((2,)),
            DMA((groups,)),
            DMA,
            DMA((6,)),
        ],
        compiler_params=pltpu.CompilerParams(
            collective_id=0, has_side_effects=True, vmem_limit_bytes=vmem
        ),
    )(positive, queries.reshape(ROWS, dim), slot_order.reshape(1, docs), queue.reshape(rows, dim))
    return loss.reshape(()), grad.reshape(1, ROWS, dim)


def solution(mesh):
    groups, tokens = mesh.shape["group"], mesh.shape["queue"]
    return jax.shard_map(
        functools.partial(on_device, groups, tokens),
        mesh=mesh,
        in_specs=(
            P("queue", "group", None),
            P(),
            P(("group", "queue"), None, None),
            P(("group", "queue")),
        ),
        out_specs=(P(), P("queue", "group", None)),
        check_vma=False,
    )
```

```python
import functools

import jax
import jax.numpy as jnp
from jax import lax
from jax.experimental import pallas as pl
from jax.experimental.pallas import tpu as pltpu
from jax.sharding import PartitionSpec as P

sharpness = 0.1
softness_divisor = 0.05
epsilon = 1e-06
log2e = 1.4426950408889634
MESH = pl.DeviceIdType.MESH
ROWS = 16
SUB = 8


def first_order(k, group):
    own = lax.div(4 - k, 4)
    other = (k - 1) + lax.div(k + 3 - group, 4)
    return own * group + (1 - own) * other


def last_order(k, group, groups):
    own = lax.div(k, groups - 1)
    other = k + lax.div(k - group + 4, 4)
    return own * group + (1 - own) * other


def kernel(
    groups, tokens, docs, length, chunks, vmem,
    pos_in, q_in, slot_in, queue_ref,
    grad_ref, loss_ref,
    pos_ref, q_ref, slot_ref, powered, doc, doc_t, qbuf, sums, logits, slot_col, st1, st2, stats, fin, gsend, grecv, yrecv,
    small_sem, load_sem, qy_recv, q_recv, s1_recv, s2_recv, s_recv, g_recv, y_recv, send_sem,
):
    group = lax.axis_index("group")
    me = lax.axis_index("queue")
    rows = docs * length
    half = tokens // 2
    lanes = half * ROWS
    chunk = rows // chunks
    blocks = 8
    block_rows = rows // blocks
    block_docs = docs // blocks
    everyone = groups * tokens
    early = groups - 2
    few = 2 * groups
    chips = tokens // 2
    core = lax.rem(me, 2)

    def load(c):
        part = pl.ds(c * chunk, chunk)
        return pltpu.make_async_copy(queue_ref.at[part], doc.at[part], load_sem.at[c])

    small = [
        pltpu.make_async_copy(src, dst, small_sem.at[n])
        for n, (src, dst) in enumerate(((q_in, q_ref), (slot_in, slot_ref), (pos_in, pos_ref)))
    ]
    for copy in small:
        copy.start()

    def peer_of(j):
        return lax.rem(me + j, tokens)

    def other_group(j):
        return lax.rem(group + j, groups)

    barrier = pltpu.get_barrier_semaphore()

    def hops(j):
        x, z = j % 8 // 2, j // 8 % 4
        return min(x, 4 - x) + min(z, 4 - z)

    around = sorted(range(1, tokens), key=hops, reverse=True)
    for j in around:
        pl.semaphore_signal(barrier, inc=1, device_id={"queue": peer_of(j)}, device_id_type=MESH)
    for j in range(1, groups):
        pl.semaphore_signal(barrier, inc=1, device_id={"group": other_group(j)}, device_id_type=MESH)
    for c in range(chunks):
        load(c).start()
    for copy in small:
        copy.wait()

    wide = q_ref[...].astype(jnp.float32)
    q_length = jnp.sqrt(jnp.sum(wide * wide, axis=-1, keepdims=True) + epsilon)
    q_unit = wide / q_length
    qbuf[group * tokens + me] = q_unit.astype(jnp.bfloat16)
    slot_col[...] = jnp.broadcast_to(slot_ref[...].astype(jnp.float32), (128, docs)).T

    pl.semaphore_wait(barrier, tokens - 1 + groups - 1)

    def to_group(src, dst, send, recv, j):
        return pltpu.make_async_remote_copy(
            src_ref=src, dst_ref=dst, send_sem=send, recv_sem=recv,
            device_id={"group": j}, device_id_type=MESH,
        )

    def to_peer(src, dst, send, recv, j):
        return pltpu.make_async_remote_copy(
            src_ref=src, dst_ref=dst, send_sem=send, recv_sem=recv,
            device_id={"queue": j}, device_id_type=MESH,
        )

    def wait_in(ref, sem):
        to_peer(ref, ref, send_sem.at[0], sem, me).wait_recv()

    def wait_out(ref, sem):
        to_peer(ref, ref, sem, q_recv.at[0], me).wait_send()

    mine = qbuf.at[group * tokens + me]
    for j in range(1, groups):
        to_group(mine, mine, send_sem.at[0], qy_recv.at[group], other_group(j)).start()

    mine_half = lax.div(me, half)
    near = [mine_half * half + lax.rem(me - mine_half * half + j, half) for j in sorted(range(1, half), key=hops, reverse=True)]
    far = [(1 - mine_half) * half + lax.rem(me - mine_half * half + j, half) for j in range(half)]

    def spread(g):
        block = qbuf.at[g * tokens + me]
        for peer in near + far:
            to_peer(block, block, send_sem.at[0], q_recv.at[2 * g + mine_half], peer).start()

    spread(group)

    def normalize(c):
        load(c).wait()
        part = pl.ds(c * chunk, chunk)
        x = doc[part, :].astype(jnp.float32)
        y = x * lax.rsqrt(jnp.sum(x * x, axis=-1, keepdims=True) + epsilon)
        y = y.reshape(chunk // (SUB * length), SUB, length, 128).swapaxes(1, 2).reshape(chunk, 128)
        doc[part, :] = y.astype(jnp.bfloat16)
        doc_t[:, part] = y.T.astype(jnp.bfloat16)

    for c in range(chunks):
        normalize(c)

    for k in range(groups - 1):
        g = last_order(k, group, groups)
        wait_in(qbuf.at[g * tokens + me], qy_recv.at[g])
        spread(g)

    lane = lax.broadcasted_iota(jnp.int32, (1, 128), 1)
    spot = lax.rem(lane, ROWS)
    field = lax.div(lane, ROWS)

    def hits(g):
        wanted = jnp.zeros((1, 128), jnp.float32)
        for b in range(ROWS):
            wanted = jnp.where(spot == b, pos_ref[g * ROWS + b].astype(jnp.float32), wanted)
        return slot_col[...] == wanted

    def everywhere(x):
        for shift in (16, 32, 64):
            x = x + pltpu.roll(x, shift, 1)
        return x

    def dots(t):
        q = qbuf[pl.ds(t * half, half)].reshape(lanes, 128).T
        for c in range(blocks):
            part = pl.ds(c * block_rows, block_rows)
            x = jnp.dot(doc[part, :], q, preferred_element_type=jnp.float32)
            e = jnp.exp2(x * (log2e / sharpness))
            powered[t, part, :] = e.astype(jnp.bfloat16)
            summed = jnp.sum(e.reshape(block_docs // SUB, length, SUB, lanes), axis=1)
            sums[t, c * block_docs:(c + 1) * block_docs, :] = summed.reshape(block_docs, lanes)

    def scores(g):
        total = jnp.zeros((docs, 128), jnp.float32)
        for h in range(2):
            score = jnp.log(sums[2 * g + h])
            for c in range(lanes // 128):
                total = total + score[:, c * 128:(c + 1) * 128]
        total = everywhere(total) * (sharpness / softness_divisor)
        logits[g] = total
        top = jnp.max(total, axis=0, keepdims=True)
        mass = jnp.sum(jnp.exp(total - top), axis=0, keepdims=True)
        target = jnp.sum(jnp.where(hits(g), total, 0.0), axis=0, keepdims=True)
        row = jnp.where(field == 0, top, 0.0)
        row = jnp.where(field == 4, mass, row)
        st1[g * few + group * 2 + core] = jnp.where(field == 5, target, row)

    def send_stats(g):
        block = st1.at[g * few + group * 2 + core]
        for i in range(groups):
            for j in range(2):
                if i + j > 0:
                    pltpu.make_async_remote_copy(
                        src_ref=block, dst_ref=block, send_sem=send_sem.at[1], recv_sem=s1_recv.at[g],
                        device_id=(other_group(i), me + j * (1 - 2 * core)), device_id_type=MESH,
                    ).start()

    def combine(parts):
        parts = parts.reshape(parts.shape[0], 128)
        top = jnp.max(parts, axis=0, keepdims=True)
        scale = jnp.exp(pltpu.roll(parts, 64, 1) - pltpu.roll(top, 64, 1))
        return jnp.where(field < 4, top, jnp.sum(parts * scale, axis=0, keepdims=True))

    def combine_column(g):
        wait_in(st1.at[pl.ds(0, few - 1)], s1_recv.at[g])
        row = g * chips + lax.div(me, 2)
        st2[row] = combine(st1[pl.ds(g * few, few)])
        block = st2.at[row]
        for j in range(1, chips):
            to_peer(block, block, send_sem.at[2], s2_recv.at[g], peer_of(2 * j)).start()

    def combine_plane(g):
        wait_in(st2.at[pl.ds(0, chips - 1)], s2_recv.at[g])
        fin[g] = combine(st2[pl.ds(g * chips, chips)])

    def send_all(g):
        row = (g - early) * everyone + group * tokens + me
        stats[row] = st1[g * few + group * 2 + core]
        block = stats.at[row]
        steps = [(i, j) for i in range(groups) for j in range(tokens) if i + j > 0]
        for i, j in sorted(steps, key=lambda s: hops(s[1]) + min(s[0], groups - s[0]), reverse=True):
            pltpu.make_async_remote_copy(
                src_ref=block, dst_ref=block, send_sem=send_sem.at[5], recv_sem=s_recv.at[g - early],
                device_id=(other_group(i), peer_of(j)), device_id_type=MESH,
            ).start()

    def combine_all(g):
        wait_in(stats.at[pl.ds(0, everyone - 1)], s_recv.at[g - early])
        fin[g] = combine(stats[pl.ds((g - early) * everyone, everyone)])

    def wait_near(t):
        wait_in(qbuf.at[pl.ds(0, half - 1)], q_recv.at[t])

    def wait_far(t):
        wait_in(qbuf.at[pl.ds(0, half)], q_recv.at[t])

    def own_tile(i, carry):
        t = 2 * group + lax.rem(mine_half + i, 2)

        @pl.when(i == 0)
        def _():
            wait_near(t)

        @pl.when(i == 1)
        def _():
            wait_far(t)

        dots(t)
        return carry

    def pass_a(k, carry):
        g = first_order(k, group)
        before = first_order(k - 1, group)
        wait_near(2 * g + mine_half)
        wait_far(2 * g + 1 - mine_half)
        scores(before)
        send_stats(before)
        dots(2 * g)
        dots(2 * g + 1)

        @pl.when(k == groups - 2)
        def _():
            combine_column(jnp.int32(0))

        return carry

    lax.fori_loop(0, 2, own_tile, 0)
    lax.fori_loop(1, groups, pass_a, 0)
    final = first_order(jnp.int32(groups - 1), group)
    combine_column(jnp.int32(1))
    scores(final)
    send_stats(final)
    send_all(early)
    send_all(early + 1)

    def gradient(t, c):
        c = jnp.concatenate([c] * (lanes // 128), axis=1) / sums[t]
        out = jnp.zeros((128, lanes), jnp.float32)
        for b in range(blocks):
            part = pl.ds(b * block_rows, block_rows)
            w = []
            for d in range(b * block_docs, (b + 1) * block_docs, SUB):
                twice = jnp.concatenate([c[d:d + SUB]] * 2, axis=0).astype(jnp.bfloat16)
                p = powered[t, pl.ds(d * length, SUB * length), :]
                w.append((p.reshape(length // 2, 2 * SUB, lanes) * twice[None]).reshape(SUB * length, lanes))
            w = jnp.concatenate(w, axis=0)
            out = out + jnp.dot(doc_t[:, part], w, preferred_element_type=jnp.float32)
        gsend[pl.ds(t * half, half)] = out.T.reshape(half, ROWS, 128).astype(jnp.bfloat16)

    def send_grad(g, peers):
        for peer in peers:
            to_peer(
                gsend.at[g * tokens + peer], grecv.at[g * tokens + me], send_sem.at[3], g_recv.at[g], peer
            ).start()

    def plane_sum(g):
        wait_in(grecv.at[pl.ds(0, tokens - 1)], g_recv.at[g])
        return jnp.sum(grecv[pl.ds(g * tokens, tokens)].astype(jnp.float32), axis=0)

    rest = groups - 1 - group
    pivot = group + rest * lax.div(rest, 2)

    def pass_b(k, carry):
        g = last_order(k, pivot, groups)


        @pl.when(g < early)
        def _():
            combine_plane(g)

        @pl.when(g >= early)
        def _():
            combine_all(g)

        row = fin[g]
        lse = everywhere(jnp.where(field == 0, row + jnp.log(pltpu.roll(row, 64, 1)), 0.0))
        c = (jnp.exp(logits[g] - lse) - hits(g).astype(jnp.float32)) / softness_divisor
        gradient(2 * g + 1 - mine_half, c)
        gradient(2 * g + mine_half, c)
        grecv[g * tokens + me] = gsend[g * tokens + me]
        send_grad(g, far + near)
        return carry

    lax.fori_loop(0, groups, pass_b, 0)

    def hand_over(k, carry):
        g = last_order(k, group, groups)
        block = yrecv.at[group * groups + g]
        yrecv[group * groups + g] = plane_sum(g)
        to_group(block, block, send_sem.at[4], y_recv, g).start()
        return carry

    lax.fori_loop(0, groups - 1, hand_over, 0)

    loss = jnp.zeros((1, 128), jnp.float32)
    for g in range(groups):
        row = fin[g]
        loss = loss + (row + jnp.log(pltpu.roll(row, 64, 1)) - pltpu.roll(row, 48, 1))
    loss = jnp.sum(jnp.where(field == 0, loss, 0.0), axis=1, keepdims=True)
    loss_ref[...] = loss * (1.0 / (groups * ROWS))

    grad = plane_sum(group)
    if groups > 1:
        wait_in(yrecv.at[pl.ds(0, groups - 1)], y_recv)
        for j in range(1, groups):
            grad = grad + yrecv[other_group(j) * groups + group]
    along = jnp.sum(q_unit * grad, axis=-1, keepdims=True)
    grad_ref[...] = (grad - q_unit * along) / q_length

    for g in range(early, groups):
        wait_in(st1.at[pl.ds(0, few - 1)], s1_recv.at[g])
    many = groups * (tokens - 1)
    wait_out(qbuf.at[pl.ds(0, many + groups - 1)], send_sem.at[0])
    wait_out(st1.at[pl.ds(0, groups * (few - 1))], send_sem.at[1])
    wait_out(st2.at[pl.ds(0, early * (chips - 1))], send_sem.at[2])
    wait_out(stats.at[pl.ds(0, 2 * (everyone - 1))], send_sem.at[5])
    wait_out(gsend.at[pl.ds(0, many)], send_sem.at[3])
    if groups > 1:
        wait_out(yrecv.at[pl.ds(0, groups - 1)], send_sem.at[4])


def on_device(groups, tokens, queries, positive, queue, slot_order):
    docs, length, dim = queue.shape
    rows = docs * length
    half = tokens // 2
    lanes = half * ROWS
    vmem = 63 * 2**20
    VM = pl.BlockSpec(memory_space=pltpu.VMEM)
    chunks = 8 if docs % 8 == 0 else 1
    f32, bf16 = jnp.float32, jnp.bfloat16
    DMA = pltpu.SemaphoreType.DMA
    grad, loss = pl.pallas_call(
        functools.partial(kernel, groups, tokens, docs, length, chunks, vmem),
        out_shape=(jax.ShapeDtypeStruct((ROWS, dim), f32), jax.ShapeDtypeStruct((1, 1), f32)),
        in_specs=[pl.BlockSpec(memory_space=pl.ANY)] * 4,
        out_specs=(VM, VM),
        scratch_shapes=[
            pltpu.SMEM((groups * ROWS,), jnp.int32),
            pltpu.VMEM((ROWS, dim), bf16),
            pltpu.VMEM((1, docs), jnp.int32),
            pltpu.VMEM((2 * groups, rows, lanes), bf16),
            pltpu.VMEM((rows, dim), bf16),
            pltpu.VMEM((dim, rows), bf16),
            pltpu.VMEM((groups * tokens, ROWS, dim), bf16),
            pltpu.VMEM((2 * groups, docs, lanes), f32),
            pltpu.VMEM((groups, docs, 128), f32),
            pltpu.VMEM((docs, 128), f32),
            pltpu.VMEM((groups * groups * 2, 1, 128), f32),
            pltpu.VMEM((groups * (tokens // 2), 1, 128), f32),
            pltpu.VMEM((2 * groups * tokens, 1, 128), f32),
            pltpu.VMEM((groups, 1, 128), f32),
            pltpu.VMEM((groups * tokens, ROWS, dim), bf16),
            pltpu.VMEM((groups * tokens, ROWS, dim), bf16),
            pltpu.VMEM((groups * groups, ROWS, dim), f32),
            DMA((3,)),
            DMA((chunks,)),
            DMA((groups,)),
            DMA((2 * groups,)),
            DMA((groups,)),
            DMA((groups,)),
            DMA((2,)),
            DMA((groups,)),
            DMA,
            DMA((6,)),
        ],
        compiler_params=pltpu.CompilerParams(
            collective_id=0, has_side_effects=True, vmem_limit_bytes=vmem
        ),
    )(positive, queries.reshape(ROWS, dim), slot_order.reshape(1, docs), queue.reshape(rows, dim))
    return loss.reshape(()), grad.reshape(1, ROWS, dim)


def solution(mesh):
    groups, tokens = mesh.shape["group"], mesh.shape["queue"]
    return jax.shard_map(
        functools.partial(on_device, groups, tokens),
        mesh=mesh,
        in_specs=(
            P("queue", "group", None),
            P(),
            P(("group", "queue"), None, None),
            P(("group", "queue")),
        ),
        out_specs=(P(), P("queue", "group", None)),
        check_vma=False,
    )
```
